512 devices in a mesh: fsdp: 32 (over z, core), tensor: 16 (over y, x).
Axes of the slice: x: 4, y: 4, z: 16, core: 2. Of those that a mesh axis runs over, the one named last changes fastest.
Arguments:
- gradient: bfloat16 [4, 1024, 8192], P(None, 'tensor', 'fsdp'), may hold values from -6 to 6
- block_owner: int32 [4, 8], replicated, may hold values from 0 to 31, as said below
- left_stats: float32 [96, 1024, 1024], P('fsdp', 'tensor'), may hold values from -6 to 6
- right_stats: float32 [96, 1024, 1024], P('fsdp', 'tensor'), may hold values from -6 to 6
- left_root: bfloat16 [96, 1024, 1024], P('fsdp', 'tensor'), may hold values from -120 to 120, as said below
- right_root: bfloat16 [96, 1024, 1024], P('fsdp', 'tensor'), may hold values from -120 to 120, as said below
Outputs:
- left_updated: float32 [96, 1024, 1024], P('fsdp', 'tensor')
- right_updated: float32 [96, 1024, 1024], P('fsdp', 'tensor')
- update: bfloat16 [4, 1024, 8192], P(None, 'tensor', 'fsdp')
The draws below stay inside these ranges and needn't reach their ends.
Inputs may be any that keep to these rules, and one draw needn't show every extreme that they name: `block_owner`: each owner holds at most 3 blocks and never two with the same row block k; some owner holds exactly 3. `left_root`: each matrix is symmetric. `right_root`: each matrix is symmetric.
All inputs are finite; a program needn't handle non-finite values.
Results may differ from the reference program's by a relative error of at most 0.0049.
Values may be sent and summed in bfloat16 or wider, within the bound.
No kernel may reach another device: no remote copies, remote signals or barrier semaphores. Data moves between devices by JAX's collectives and lax.ppermute only.
A program may use at most 64 MiB of HBM per device.

```python
import math
import jax
import jax.numpy as jnp
import numpy as np
from jax import lax

ROWS = 8192
BS = 1024
CAP = 3
NRB = 8
NCB = 4
NB = 32
SLOTS = 96


LOAD_PATTERNS = np.array([[0, 0, 0, 1, 1, 2, 3, 4], [0, 0, 0, 1, 2, 3, 4, 5], [0, 0, 0, 1, 1, 2, 2, 3]], dtype=np.int32)


def draw_block_owner(key, part):
    key = jax.random.fold_in(key, 11)
    keys = jax.random.split(key, 5)
    pattern_pick = jax.random.randint(keys[0], (NCB,), 0, 3)
    patterns = jnp.asarray(LOAD_PATTERNS)[pattern_pick]
    placing = jax.vmap(lambda subkey: jax.random.permutation(subkey, NRB))(jax.random.split(keys[1], NCB))
    labels = jax.vmap(lambda subkey: jax.random.permutation(subkey, NRB))(jax.random.split(keys[2], NCB))
    heights = jnp.take_along_axis(labels, jnp.take_along_axis(patterns, placing, axis=1), axis=1)
    shifts = jax.random.randint(keys[3], (NRB,), 0, NCB)
    columns = jnp.arange(NCB)[:, None]
    bands = jnp.arange(NRB)[None, :]
    virtual = (columns + shifts[None, :]) % NCB
    levels = heights[virtual, bands]
    slot_owner = virtual + NCB * levels
    relabel = jax.random.permutation(keys[4], NCB * NRB)
    return relabel[slot_owner].astype(jnp.int32)


def shape_root(noise, diagonal, row_scales):
    offdiag = (noise + jnp.swapaxes(noise, 1, 2)) * (0.35 / math.sqrt(BS))
    identity = jnp.eye(BS, dtype=jnp.float32)
    core = offdiag * (1.0 - identity) + identity * diagonal[:, :, None]
    rising = 3.0 ** (jnp.arange(BS, dtype=jnp.float32) / BS)
    scales = row_scales * rising[None, :]
    return core * jnp.sqrt(scales[:, :, None] * scales[:, None, :])


def draw_left_root(key, part):
    key = jax.random.fold_in(key, 21)
    keys = jax.random.split(key, 3)
    noise = jax.random.normal(keys[0], (SLOTS, BS, BS), jnp.float32)
    diagonal = jax.random.uniform(keys[1], (SLOTS, BS), jnp.float32, 0.5, 1.5)
    row_scales = jnp.exp(jax.random.uniform(keys[2], (SLOTS, BS), jnp.float32, 0.0, math.log(10.0)))
    return shape_root(noise, diagonal, row_scales).astype(jnp.bfloat16)


def draw_right_root(key, part):
    key = jax.random.fold_in(key, 22)
    keys = jax.random.split(key, 3)
    noise = jax.random.normal(keys[0], (SLOTS, BS, BS), jnp.float32)
    diagonal = jax.random.uniform(keys[1], (SLOTS, BS), jnp.float32, 0.5, 1.5)
    row_scales = jnp.exp(jax.random.uniform(keys[2], (SLOTS, BS), jnp.float32, 0.0, math.log(10.0)))
    return shape_root(noise, diagonal, row_scales).astype(jnp.bfloat16)


def level_of(own_key, dims, cuts, least, high):
    def one(axis_at, shards_of):
        draws = jax.random.uniform(jax.random.fold_in(jax.random.fold_in(own_key, 6), axis_at), (shards_of,), jnp.float32, least / len(cuts), high / len(cuts))
        return jnp.repeat(jnp.exp(draws), dims[axis_at] // shards_of).reshape((-1,) + (1,) * (len(dims) - axis_at - 1))

    gain = one(*cuts[0])
    for cut in cuts[1:]:
        gain = gain * one(*cut)
    return gain


def gaussian(rng, extent, deviation, limit, pieces=(), held_as=jnp.bfloat16):
    drawn = deviation * jax.random.normal(rng, extent, jnp.float32)
    if pieces:
        drawn = drawn * level_of(rng, extent, pieces, -0.22, 0.18)
    return jnp.clip(drawn, -limit, limit).astype(held_as)


def setup_inputs(seed: int = 0) -> dict:
    key_list = jax.random.split(jax.random.key(seed), 7)
    return {
        "gradient": gaussian(key_list[0], (NCB, BS, ROWS), 1.0, 6.0, ((1, 16), (2, 32))),
        "block_owner": draw_block_owner(jax.random.fold_in(key_list[6], 71), 0),
        "left_stats": gaussian(key_list[2], (SLOTS, BS, BS), 1.0, 6.0, ((0, 32), (1, 16)), jnp.float32),
        "right_stats": gaussian(key_list[3], (SLOTS, BS, BS), 1.0, 6.0, ((0, 32), (1, 16)), jnp.float32),
        "left_root": draw_left_root(jax.random.fold_in(key_list[6], 71), 0),
        "right_root": draw_right_root(jax.random.fold_in(key_list[6], 71), 0),
    }


BETA = 0.999
STEP = 0.5
EPS = 1e-06

def slot_numbers(owners_flat):
    total = owners_flat.shape[0]
    same = owners_flat[:, None] == owners_flat[None, :]
    earlier = jnp.arange(total)[None, :] < jnp.arange(total)[:, None]
    return lax.optimization_barrier(jnp.sum(jnp.where(same & earlier, 1, 0), axis=1)).astype(jnp.int32)

def reference(gradient, block_owner, left_stats, right_stats, left_root, right_root):
    blocks = gradient.reshape(NCB, BS, NRB, BS).transpose(0, 2, 1, 3).reshape(NB, BS, BS)
    owners_flat = block_owner.reshape(-1).astype(jnp.int32)
    entries = (owners_flat * CAP + slot_numbers(owners_flat)).astype(jnp.int32)

    def one_block(packed):
        block, entry = packed
        left_factor = lax.dynamic_index_in_dim(left_root, entry, 0, keepdims=False)
        right_factor = lax.dynamic_index_in_dim(right_root, entry, 0, keepdims=False)
        left_term = jnp.dot(block, block.T, preferred_element_type=jnp.float32)
        right_term = jnp.dot(block.T, block, preferred_element_type=jnp.float32)
        mixed = jnp.dot(left_factor, block, preferred_element_type=jnp.float32).astype(jnp.bfloat16)
        precond = jnp.dot(mixed, right_factor, preferred_element_type=jnp.float32)
        wide_block = block.astype(jnp.float32)
        grad_power = jnp.sum(wide_block * wide_block)
        pre_power = jnp.sum(precond * precond)
        graft_scale = -STEP * jnp.sqrt(grad_power) * lax.rsqrt(pre_power + EPS)
        return (left_term, right_term, (graft_scale * precond).astype(jnp.bfloat16))
    left_terms, right_terms, steps_done = lax.map(one_block, (blocks, entries))
    left_updated = (BETA * left_stats).at[entries].set(BETA * left_stats[entries] + (1.0 - BETA) * left_terms)
    right_updated = (BETA * right_stats).at[entries].set(BETA * right_stats[entries] + (1.0 - BETA) * right_terms)
    update = steps_done.reshape(NCB, NRB, BS, BS).transpose(0, 2, 1, 3).reshape(NCB, BS, ROWS)
    return (left_updated, right_updated, update)
```

```python
import functools
import jax
import jax.numpy as jnp
from jax import lax
from jax.experimental import pallas as pl
from jax.experimental.pallas import tpu as pltpu
from jax.sharding import PartitionSpec as P

BETA = 0.999
STEP = 0.5
EPS = 1e-06
TAIL = 16
VMEM = pl.BlockSpec(memory_space=pltpu.VMEM)
SMEM = pl.BlockSpec(memory_space=pltpu.SMEM)
LIMIT = pltpu.CompilerParams(vmem_limit_bytes=24 * 2**20)


def cost(flops, moved):
    return pl.CostEstimate(flops=flops, bytes_accessed=moved, transcendentals=0)


def slot_numbers(owners_flat):
    total = owners_flat.shape[0]
    same = owners_flat[:, None] == owners_flat[None, :]
    earlier = jnp.arange(total)[None, :] < jnp.arange(total)[:, None]
    return jnp.sum(jnp.where(same & earlier, 1, 0), axis=1).astype(jnp.int32)


def exchange(pieces):
    return lax.all_to_all(pieces, "tensor", split_axis=0, concat_axis=0, tiled=True)


def outgoing_kernel(owner_ref, gradient_ref, out_ref):
    out_ref[...] = jnp.zeros(out_ref.shape, out_ref.dtype)
    for column in range(gradient_ref.shape[0]):
        out_ref[owner_ref[column]] = gradient_ref[column]


def held_rows_kernel(band_ref, used_ref, pieces_ref, sent_ref, rows_ref, sems):
    capacity, _, block_side = rows_ref.shape
    width = pieces_ref.shape[2]
    parts = block_side // width
    copies = []
    for slot in range(capacity + 1):
        if slot < capacity:
            keep = used_ref[slot] > 0
            for part in range(parts):
                piece = pieces_ref[band_ref[slot] * parts + part]
                rows_ref[slot, :, pl.ds(part * width, width)] = jnp.where(
                    keep, piece, jnp.zeros_like(piece)
                )
        for member in range(parts):
            place = slot * parts + member
            if place < sent_ref.shape[0]:
                source = rows_ref.at[min(slot, capacity - 1)]
                copies.append(pltpu.make_async_copy(source, sent_ref.at[place], sems.at[place]))
                copies[-1].start()
    for copy in copies:
        copy.wait()


def held_rows(band_of, used, pieces, capacity, block_side, places):
    height = pieces.shape[1]
    return pl.pallas_call(
        held_rows_kernel,
        out_shape=jax.ShapeDtypeStruct((places, height, block_side), pieces.dtype),
        in_specs=[SMEM, SMEM, VMEM],
        out_specs=pl.BlockSpec(memory_space=pl.ANY),
        scratch_shapes=[
            pltpu.VMEM((capacity, height, block_side), pieces.dtype),
            pltpu.SemaphoreType.DMA((places,)),
        ],
        compiler_params=LIMIT,
        cost_estimate=cost(0, 4 * 2**20),
    )(band_of, used, pieces)


def three_parts(value):
    high = value.astype(jnp.bfloat16)
    rest = value - high.astype(jnp.float32)
    middle = rest.astype(jnp.bfloat16)
    return [high, middle, (rest - middle.astype(jnp.float32)).astype(jnp.bfloat16)]


def around(place, step, count):
    return lax.rem(place + count - step, count)


def precondition_kernel(side, place_ref, *refs):
    left_refs, (right_ref, block_ref, out_ref) = refs[:side], refs[side:]
    y, x = place_ref[0], place_ref[1]
    places, height, block_side = block_ref.shape
    width = out_ref.shape[2]
    block = block_ref[...].reshape(block_side, block_side)
    right = jnp.concatenate([right_ref[around(y, at, side)] for at in range(side)], axis=0)
    power = jnp.zeros((1, width), jnp.float32)
    for step in range(side):
        left = left_refs[step][...].reshape(side * height, block_side)
        mixed = jnp.dot(left, block, preferred_element_type=jnp.float32).astype(jnp.bfloat16)
        product = lax.dot_general(
            mixed, right, (((1,), (1,)), ((), ())), preferred_element_type=jnp.float32
        )
        power += jnp.sum(product * product, axis=0, keepdims=True)
        product = product.astype(jnp.bfloat16)
        for at in range(side):
            place = around(y, at, side) * side + around(x, step, side)
            out_ref[place, pl.ds(0, height), :] = product[at * height : (at + 1) * height]
    share = places // side
    own = block_ref[pl.ds(x * share, share)].astype(jnp.float32).reshape(width, block_side)
    own = jnp.sum(own * own, axis=0, keepdims=True)
    grad = sum(own[:, at * width : (at + 1) * width] for at in range(side))
    number = lax.broadcasted_iota(jnp.int32, (TAIL, width), 0)
    tail = jnp.zeros((TAIL, width), jnp.float32)
    for at, line in enumerate(three_parts(power) + three_parts(grad)):
        tail = jnp.where(number == at, line.astype(jnp.float32), tail)
    tail = tail.astype(jnp.bfloat16)
    for place in range(places):
        out_ref[place, pl.ds(height, TAIL), :] = tail


def precondition(place, lefts, right, block):
    places, height, block_side = block.shape
    width = block_side // len(lefts)
    return pl.pallas_call(
        functools.partial(precondition_kernel, len(lefts)),
        out_shape=jax.ShapeDtypeStruct((places, height + TAIL, width), jnp.bfloat16),
        in_specs=[SMEM] + [VMEM] * (len(lefts) + 2),
        out_specs=VMEM,
        compiler_params=pltpu.CompilerParams(vmem_limit_bytes=32 * 2**20),
        cost_estimate=cost(2 * block_side * block_side * (block_side + width), 6 * 2**20),
    )(place, *lefts, right, block)


def steps_kernel(side, band_ref, used_ref, back_ref, out_ref):
    height, width = out_ref.shape[1:]
    piece = width // side
    out_ref[...] = jnp.zeros(out_ref.shape, out_ref.dtype)
    for slot in range(band_ref.shape[0]):
        sums = sum(
            back_ref[slot * side + member, pl.ds(height, TAIL), :].astype(jnp.float32)
            for member in range(side)
        )
        sums = jnp.sum(sums, axis=1, keepdims=True)
        power = jnp.sum(sums[0:3], axis=0, keepdims=True)
        grad = jnp.sum(sums[3:6], axis=0, keepdims=True)
        scale = -STEP * jnp.sqrt(grad) * lax.rsqrt(power + EPS)

        @pl.when(used_ref[slot] > 0)
        def _():
            parts = [
                (
                    scale * back_ref[slot * side + member, pl.ds(0, height), :].astype(jnp.float32)
                ).astype(jnp.bfloat16)
                for member in range(side)
            ]
            for part in range(side):
                out_ref[band_ref[slot] * side + part] = jnp.concatenate(
                    [rows[:, part * piece : (part + 1) * piece] for rows in parts], axis=1
                )


def update_kernel(owner_ref, returned_ref, out_ref):
    for column in range(out_ref.shape[0]):
        out_ref[column] = returned_ref[owner_ref[column]]


def statistics_kernel(side, place_ref, left_ref, right_ref, *refs):
    term_refs, outs = refs[:side], refs[side:]
    y, x = place_ref[0], place_ref[1]
    width = left_ref.shape[2] // side
    for step in range(side):
        columns = pl.ds(pl.multiple_of(around(x, step, side) * width, width), width)
        for slot in range(left_ref.shape[0]):
            for kind, (old, new) in enumerate(zip((left_ref, right_ref), outs)):
                term = term_refs[step][around(y, slot, side), kind].astype(jnp.float32)
                new[slot, :, columns] = BETA * old[slot, :, columns] + (1.0 - BETA) * term


def per_device(gradient, block_owner, left_stats, right_stats, left_root, right_root):
    tensor_index = lax.axis_index("tensor")
    fsdp_index = lax.axis_index("fsdp")
    fsdp_count = lax.axis_size("fsdp")
    tensor_count = lax.axis_size("tensor")
    col_blocks, local_height, row_depth = gradient.shape
    row_blocks = block_owner.shape[1]
    capacity, _, block_side = left_stats.shape
    side = block_side // row_depth
    y, x = tensor_index // side, tensor_index % side
    place = jnp.stack([y, x]).astype(jnp.int32)

    def along_y(value, step, sources, targets):
        pairs = [
            (a * side + b, (a + step) % side * side + b)
            for a in range(side)
            for b in range(side)
            if a < sources and (a + step) % side < targets
        ]
        return lax.ppermute(value, "tensor", pairs)

    def along_x(value, step, rows):
        pairs = [
            (a * side + b, a * side + (b + step) % side) for a in range(rows) for b in range(side)
        ]
        return lax.ppermute(value, "tensor", pairs)

    with jax.named_scope("gradient_to_owners"):
        band_mask = jnp.arange(row_blocks) == fsdp_index // side
        band_owner = jnp.sum(jnp.where(band_mask[None, :], block_owner, 0), axis=1)
        band_owner = band_owner.astype(jnp.int32)
        outgoing = pl.pallas_call(
            outgoing_kernel,
            out_shape=jax.ShapeDtypeStruct((fsdp_count, local_height, row_depth), gradient.dtype),
            in_specs=[SMEM, VMEM],
            out_specs=VMEM,
            compiler_params=LIMIT,
            cost_estimate=cost(0, 2**20),
        )(band_owner, gradient)
        outgoing, left_root, right_root = lax.optimization_barrier(
            (outgoing, left_root, right_root)
        )
        pieces = lax.all_to_all(outgoing, "fsdp", split_axis=0, concat_axis=0, tiled=True)

    with jax.named_scope("roots_to_slot_groups"):
        roots = jnp.stack([left_root, right_root], axis=1)
        taken = []
        for step in range(side):
            slot = jnp.minimum((y + step) % side, capacity - 1)
            own = lax.dynamic_index_in_dim(roots, slot, 0, keepdims=False)
            taken.append(along_y(own, step, side, capacity) if step else own)
        left_rows = jnp.stack([piece[0] for piece in taken])
        right_rows = jnp.stack([piece[1] for piece in taken])
        lefts = [left_rows] + [along_x(left_rows, step, capacity) for step in range(1, side)]
        pieces, right_rows, *lefts = lax.optimization_barrier((pieces, right_rows, *lefts))

    with jax.named_scope("held_blocks"):
        owners_flat = block_owner.reshape(-1)
        numbers = jnp.arange(owners_flat.shape[0])
        held = (owners_flat == fsdp_index)[:, None] & (
            slot_numbers(owners_flat)[:, None] == jnp.arange(capacity)[None, :]
        )
        used = jnp.any(held, axis=0).astype(jnp.int32)
        band_of = jnp.sum(jnp.where(held, (numbers % row_blocks)[:, None], 0), axis=0)
        band_of = band_of.astype(jnp.int32)

    with jax.named_scope("rows_of_held_blocks"):
        block = exchange(held_rows(band_of, used, pieces, capacity, block_side, tensor_count))

    with jax.named_scope("precondition"):
        leaving = precondition(place, lefts, right_rows, block)

    with jax.named_scope("step_to_gradient_rows"):
        back = exchange(leaving)
        steps = pl.pallas_call(
            functools.partial(steps_kernel, side),
            out_shape=jax.ShapeDtypeStruct((fsdp_count, local_height, row_depth), jnp.bfloat16),
            in_specs=[SMEM, SMEM, VMEM],
            out_specs=VMEM,
            compiler_params=LIMIT,
            cost_estimate=cost(0, 2 * 2**20),
        )(band_of, used, back)
        returned = lax.all_to_all(steps, "fsdp", split_axis=0, concat_axis=0, tiled=True)

    with jax.named_scope("statistics"):
        block, steps = lax.optimization_barrier((block, steps))
        block = block.reshape(block_side, block_side)
        chunk_rows = lax.dynamic_slice_in_dim(block, x * row_depth, row_depth, 0)
        chunk_columns = lax.dynamic_slice_in_dim(block, x * row_depth, row_depth, 1)
        left_term = jnp.einsum("jk,ck->jc", block, chunk_rows, preferred_element_type=jnp.float32)
        right_term = jnp.einsum(
            "jk,jc->kc", block, chunk_columns, preferred_element_type=jnp.float32
        )
        terms = jnp.stack([left_term.astype(jnp.bfloat16), right_term.astype(jnp.bfloat16)])
        terms = terms.reshape(2, side, block_side // side, row_depth)
        gathered = []
        for step in range(side):
            own = lax.dynamic_index_in_dim(terms, (y + step) % side, 1, keepdims=False)
            gathered.append(along_y(own, step, capacity, side) if step else own)
        gathered = jnp.stack(gathered).reshape(side, 2, side, local_height, row_depth)
        arrived = []
        for step in range(side):
            own = lax.dynamic_index_in_dim(gathered, (x + step) % side, 2, keepdims=False)
            arrived.append(along_x(own, step, side) if step else own)
        left_updated, right_updated = pl.pallas_call(
            functools.partial(statistics_kernel, side),
            out_shape=(
                jax.ShapeDtypeStruct(left_stats.shape, left_stats.dtype),
                jax.ShapeDtypeStruct(right_stats.shape, right_stats.dtype),
            ),
            in_specs=[SMEM] + [VMEM] * (2 + side),
            out_specs=(VMEM, VMEM),
            compiler_params=LIMIT,
            cost_estimate=cost(0, 4 * 2**20),
        )(place, left_stats, right_stats, *arrived)
        returned, left_updated, right_updated = lax.optimization_barrier(
            (returned, left_updated, right_updated)
        )

    with jax.named_scope("update"):
        update = pl.pallas_call(
            update_kernel,
            out_shape=jax.ShapeDtypeStruct(gradient.shape, gradient.dtype),
            in_specs=[SMEM, VMEM],
            out_specs=VMEM,
            compiler_params=LIMIT,
            cost_estimate=cost(0, 2**20),
        )(band_owner, returned)
    return (left_updated, right_updated, update)


def solution(mesh):
    placed = (
        P(None, "tensor", "fsdp"),
        P(),
        P("fsdp", "tensor", None),
        P("fsdp", "tensor", None),
        P("fsdp", "tensor", None),
        P("fsdp", "tensor", None),
    )
    return jax.shard_map(
        per_device,
        mesh=mesh,
        in_specs=placed,
        out_specs=(P("fsdp", "tensor", None), P("fsdp", "tensor", None), P(None, "tensor", "fsdp")),
        check_vma=False,
    )
```

```python
import functools
import jax
import jax.numpy as jnp
from jax import lax
from jax.experimental import pallas as pl
from jax.experimental.pallas import tpu as pltpu
from jax.sharding import PartitionSpec as P

BETA = 0.999
STEP = 0.5
EPS = 1e-06
TAIL = 16
ROWS = 16
LANES = 128
VMEM = pl.BlockSpec(memory_space=pltpu.VMEM)
ANY = pl.BlockSpec(memory_space=pl.ANY)
SMEM = pl.BlockSpec(memory_space=pltpu.SMEM)
LIMIT = pltpu.CompilerParams(vmem_limit_bytes=24 * 2**20)


def cost(flops, moved):
    return pl.CostEstimate(flops=flops, bytes_accessed=moved, transcendentals=0)


def slot_numbers(owners_flat):
    total = owners_flat.shape[0]
    same = owners_flat[:, None] == owners_flat[None, :]
    earlier = jnp.arange(total)[None, :] < jnp.arange(total)[:, None]
    return jnp.sum(jnp.where(same & earlier, 1, 0), axis=1).astype(jnp.int32)


def exchange(pieces):
    return lax.all_to_all(pieces, "tensor", split_axis=0, concat_axis=0, tiled=True)


def tile_of(number):
    return pl.ds(number // 2 * ROWS, ROWS), pl.ds(number % 2 * LANES, LANES)


def spread_kernel(part_ref, gradient_ref, out_ref):
    count = gradient_ref.shape[0]
    tiles = out_ref.shape[0] // count
    for group in range(count):
        column = lax.rem(group + count - part_ref[0], count)
        for tile in range(tiles):
            rows, lanes = tile_of(tile)
            out_ref[group * tiles + tile] = gradient_ref[column, rows, lanes]


def pick_kernel(index_ref, tiles_ref, out_ref):
    for at in range(out_ref.shape[0]):
        out_ref[at] = tiles_ref[index_ref[at]]


def pick(index, tiles):
    shape = (index.shape[0],) + tiles.shape[1:]
    return pl.pallas_call(
        pick_kernel,
        out_shape=jax.ShapeDtypeStruct(shape, tiles.dtype),
        in_specs=[SMEM, VMEM],
        out_specs=VMEM,
        compiler_params=LIMIT,
        cost_estimate=cost(0, 2**20),
    )(index, tiles)


def held_rows_kernel(column_ref, used_ref, tiles_ref, sent_ref, rows_ref, sems):
    capacity, _, block_side = rows_ref.shape
    places = sent_ref.shape[0]
    parts = places // (capacity + 1)
    width = block_side // parts
    tiles = tiles_ref.shape[0] // parts
    copies = []
    for slot in range(capacity + 1):
        if slot < capacity:
            keep = used_ref[slot] > 0
            for part in range(parts):
                group = lax.rem(column_ref[slot] + part, parts)
                for tile in range(tiles):
                    rows, lanes = tile_of(tile)
                    lanes = pl.ds(part * width + lanes.start, LANES)
                    value = tiles_ref[group * tiles + tile, slot]
                    rows_ref[slot, rows, lanes] = jnp.where(keep, value, jnp.zeros_like(value))
        for member in range(parts):
            place = slot * parts + member
            source = rows_ref.at[min(slot, capacity - 1)]
            copies.append(pltpu.make_async_copy(source, sent_ref.at[place], sems.at[place]))
            copies[-1].start()
    for copy in copies:
        copy.wait()


def held_rows(column_of, used, tiles, height, block_side, places):
    capacity = tiles.shape[1]
    return pl.pallas_call(
        held_rows_kernel,
        out_shape=jax.ShapeDtypeStruct((places, height, block_side), tiles.dtype),
        in_specs=[SMEM, SMEM, VMEM],
        out_specs=ANY,
        scratch_shapes=[
            pltpu.VMEM((capacity, height, block_side), tiles.dtype),
            pltpu.SemaphoreType.DMA((places,)),
        ],
        compiler_params=LIMIT,
        cost_estimate=cost(0, 4 * 2**20),
    )(column_of, used, tiles)


def three_parts(value):
    high = value.astype(jnp.bfloat16)
    rest = value - high.astype(jnp.float32)
    middle = rest.astype(jnp.bfloat16)
    return [high, middle, (rest - middle.astype(jnp.float32)).astype(jnp.bfloat16)]


def around(place, step, count):
    return lax.rem(place + count - step, count)


def precondition_kernel(side, origins, place_ref, *refs):
    left_ref, right_ref, block_ref, out_ref = refs
    y, x = place_ref[0], place_ref[1]
    places, height, block_side = block_ref.shape
    width = out_ref.shape[2]
    block = block_ref[...].reshape(block_side, block_side)
    right = jnp.concatenate([right_ref[around(y, at, side)] for at in range(side)], axis=0)
    power = jnp.zeros((1, width), jnp.float32)
    for begin in range(0, places, side):
        left = left_ref[pl.ds(begin, side)].reshape(side * height, block_side)
        mixed = jnp.dot(left, block, preferred_element_type=jnp.float32).astype(jnp.bfloat16)
        product = lax.dot_general(
            mixed, right, (((1,), (1,)), ((), ())), preferred_element_type=jnp.float32
        )
        power += jnp.sum(product * product, axis=0, keepdims=True)
        product = product.astype(jnp.bfloat16)
        for at, (row, column) in enumerate(origins[begin : begin + side]):
            place = around(y, row, side) * side + around(x, column, side)
            out_ref[place, pl.ds(0, height), :] = product[at * height : (at + 1) * height]
    share = places // side
    own = block_ref[pl.ds(x * share, share)].astype(jnp.float32).reshape(width, block_side)
    own = jnp.sum(own * own, axis=0, keepdims=True)
    grad = sum(own[:, at * width : (at + 1) * width] for at in range(side))
    number = lax.broadcasted_iota(jnp.int32, (TAIL, width), 0)
    tail = jnp.zeros((TAIL, width), jnp.float32)
    for at, line in enumerate(three_parts(power) + three_parts(grad)):
        tail = jnp.where(number == at, line.astype(jnp.float32), tail)
    tail = tail.astype(jnp.bfloat16)
    for place in range(places):
        out_ref[place, pl.ds(height, TAIL), :] = tail


def precondition(place, left, origins, right, block):
    places, height, block_side = block.shape
    side = right.shape[0]
    width = block_side // side
    return pl.pallas_call(
        functools.partial(precondition_kernel, side, origins),
        out_shape=jax.ShapeDtypeStruct((places, height + TAIL, width), jnp.bfloat16),
        in_specs=[SMEM] + [VMEM] * 3,
        out_specs=VMEM,
        compiler_params=pltpu.CompilerParams(vmem_limit_bytes=32 * 2**20),
        cost_estimate=cost(2 * block_side * block_side * (block_side + width), 6 * 2**20),
    )(place, left, right, block)


def steps_kernel(side, column_ref, back_ref, out_ref):
    height = back_ref.shape[1] - TAIL
    piece = back_ref.shape[2] // side
    tiles = out_ref.shape[0] // side
    for slot in range(column_ref.shape[0]):
        sums = sum(
            back_ref[slot * side + member, pl.ds(height, TAIL), :].astype(jnp.float32)
            for member in range(side)
        )
        sums = jnp.sum(sums, axis=1, keepdims=True)
        power = jnp.sum(sums[0:3], axis=0, keepdims=True)
        grad = jnp.sum(sums[3:6], axis=0, keepdims=True)
        scale = -STEP * jnp.sqrt(grad) * lax.rsqrt(power + EPS)
        rows_of = [
            (
                scale * back_ref[slot * side + member, pl.ds(0, height), :].astype(jnp.float32)
            ).astype(jnp.bfloat16)
            for member in range(side)
        ]
        for part in range(side):
            group = lax.rem(column_ref[slot] + part, side)
            chunk = jnp.concatenate(
                [rows[:, part * piece : (part + 1) * piece] for rows in rows_of], axis=1
            )
            for tile in range(tiles):
                rows, lanes = tile_of(tile)
                out_ref[group * tiles + tile, slot] = chunk[
                    rows.start : rows.start + ROWS, lanes.start : lanes.start + LANES
                ]


def update_kernel(part_ref, tiles_ref, out_ref):
    count = out_ref.shape[0]
    tiles = tiles_ref.shape[0] // count
    for column in range(count):
        group = lax.rem(column + part_ref[0], count)
        for tile in range(tiles):
            rows, lanes = tile_of(tile)
            out_ref[column, rows, lanes] = tiles_ref[group * tiles + tile]


def statistics_kernel(side, place_ref, left_ref, right_ref, *refs):
    term_refs, outs = refs[:side], refs[side:]
    for step in range(side):
        slot = around(place_ref[0], step, side)

        @pl.when(slot < left_ref.shape[0])
        def _():
            for kind, (old, new) in enumerate(zip((left_ref, right_ref), outs)):
                term = term_refs[step][kind].astype(jnp.float32)
                new[slot] = BETA * old[slot] + (1.0 - BETA) * term


def per_device(gradient, block_owner, left_stats, right_stats, left_root, right_root):
    tensor_index = lax.axis_index("tensor")
    fsdp_index = lax.axis_index("fsdp")
    fsdp_count = lax.axis_size("fsdp")
    tensor_count = lax.axis_size("tensor")
    col_blocks, local_height, row_depth = gradient.shape
    row_blocks = block_owner.shape[1]
    capacity, _, block_side = left_stats.shape
    side = block_side // row_depth
    y, x = tensor_index // side, tensor_index % side
    place = jnp.stack([y, x]).astype(jnp.int32)

    def along_y(value, step, sources, targets):
        pairs = [
            (a * side + b, (a + step) % side * side + b)
            for a in range(side)
            for b in range(side)
            if a < sources and (a + step) % side < targets
        ]
        return lax.ppermute(value, "tensor", pairs)

    def along_x(value, step, rows):
        pairs = [
            (a * side + b, a * side + (b + step) % side) for a in range(rows) for b in range(side)
        ]
        return lax.ppermute(value, "tensor", pairs)

    def over_rows(value):
        return lax.all_to_all(value, "fsdp", split_axis=0, concat_axis=0, tiled=True)

    part = (fsdp_index % side).astype(jnp.int32).reshape(1)
    group = fsdp_index // (fsdp_count // col_blocks)

    with jax.named_scope("gradient_spread"):
        spread = pl.pallas_call(
            spread_kernel,
            out_shape=jax.ShapeDtypeStruct((fsdp_count, ROWS, LANES), gradient.dtype),
            in_specs=[SMEM, VMEM],
            out_specs=VMEM,
            compiler_params=LIMIT,
            cost_estimate=cost(0, 2**18),
        )(part, gradient)
        spread, left_root, right_root = lax.optimization_barrier((spread, left_root, right_root))
        spread = over_rows(spread)

    with jax.named_scope("where_blocks_go"):
        owners_flat = block_owner.reshape(-1)
        numbers = jnp.arange(owners_flat.shape[0])
        column_flat, band_flat = numbers // row_blocks, numbers % row_blocks
        entries = owners_flat * capacity + slot_numbers(owners_flat)
        held_at = entries[:, None] == jnp.arange(fsdp_count * capacity)[None, :]
        source = band_flat * side + (group - column_flat + side) % side
        forward = jnp.sum(jnp.where(held_at, source[:, None], 0), axis=0).astype(jnp.int32)
        mine = entries[:, None] == (fsdp_index * capacity + jnp.arange(capacity))[None, :]
        used = jnp.any(mine, axis=0).astype(jnp.int32)
        column_of = jnp.sum(jnp.where(mine, column_flat[:, None], 0), axis=0).astype(jnp.int32)
        homes = jnp.arange(fsdp_count)
        wanted = (group - homes % side + side) % side * row_blocks + homes // side
        backward = jnp.sum(
            jnp.where(wanted[:, None] == numbers[None, :], entries[None, :], 0), axis=1
        ).astype(jnp.int32)

    with jax.named_scope("gradient_to_owners"):
        sent = pick(forward, spread).reshape(fsdp_count, capacity, ROWS, LANES)
        tiles = over_rows(sent)

    with jax.named_scope("roots_to_slot_groups"):
        roots = jnp.stack([left_root, right_root], axis=1)
        taken = []
        for step in range(side):
            slot = jnp.minimum((y + step) % side, capacity - 1)
            own = lax.dynamic_index_in_dim(roots, slot, 0, keepdims=False)
            taken.append(along_y(own, step, side, capacity) if step else own)
        left_rows = jnp.stack([piece[0] for piece in taken])
        right_rows = jnp.stack([piece[1] for piece in taken])
        half = side // 2
        before = along_x(left_rows, 1, capacity)
        behind = along_x(left_rows, side - 1, capacity)
        lefts = [
            left_rows,
            before,
            behind,
            along_x(before[:half], 1, capacity),
            along_x(behind[half:], side - 1, capacity),
        ]
        origins = [
            (row, column) for column in (0, 1, side - 1, half) for row in range(side)
        ]
        tiles, right_rows, *lefts = lax.optimization_barrier((tiles, right_rows, *lefts))

    with jax.named_scope("rows_of_held_blocks"):
        sent = held_rows(column_of, used, tiles, local_height, block_side, tensor_count)
        sent, *lefts = lax.optimization_barrier((sent, *lefts))
        block = exchange(sent)
        left = jnp.concatenate(lefts)

    with jax.named_scope("precondition"):
        leaving = precondition(place, left, origins, right_rows, block)

    with jax.named_scope("step_to_gradient_rows"):
        back = exchange(leaving)
        steps = pl.pallas_call(
            functools.partial(steps_kernel, side),
            out_shape=jax.ShapeDtypeStruct((fsdp_count, capacity, ROWS, LANES), jnp.bfloat16),
            in_specs=[SMEM, VMEM],
            out_specs=VMEM,
            compiler_params=LIMIT,
            cost_estimate=cost(0, 2 * 2**20),
        )(column_of, back)
        passing = over_rows(steps).reshape(fsdp_count * capacity, ROWS, LANES)

    with jax.named_scope("statistics"):
        block, steps = lax.optimization_barrier((block, steps))
        block = block.reshape(block_side, block_side)
        own_rows = lax.dynamic_index_in_dim(
            block.reshape(side, side, local_height, block_side), x, 1, keepdims=False
        ).reshape(row_depth, block_side)
        own_columns = jnp.concatenate(
            [
                lax.dynamic_slice_in_dim(block, (at * side + x) * local_height, local_height, 1)
                for at in range(side)
            ],
            axis=1,
        )
        left_term = jnp.einsum("ak,jk->aj", own_rows, block, preferred_element_type=jnp.float32)
        right_term = jnp.einsum("ja,jk->ak", own_columns, block, preferred_element_type=jnp.float32)
        terms = jnp.stack([left_term.astype(jnp.bfloat16), right_term.astype(jnp.bfloat16)])
        terms = terms.reshape(2, side, local_height, block_side)
        arrived = []
        for step in range(side):
            own = lax.dynamic_index_in_dim(terms, (y + step) % side, 1, keepdims=False)
            arrived.append(along_y(own, step, capacity, side) if step else own)
        passing, *arrived = lax.optimization_barrier((passing, *arrived))
        returned = over_rows(pick(backward, passing))
        left_updated, right_updated = pl.pallas_call(
            functools.partial(statistics_kernel, side),
            out_shape=(
                jax.ShapeDtypeStruct(left_stats.shape, left_stats.dtype),
                jax.ShapeDtypeStruct(right_stats.shape, right_stats.dtype),
            ),
            in_specs=[SMEM] + [VMEM] * (2 + side),
            out_specs=(VMEM, VMEM),
            compiler_params=LIMIT,
            cost_estimate=cost(0, 4 * 2**20),
        )(place, left_stats, right_stats, *arrived)
        returned, left_updated, right_updated = lax.optimization_barrier(
            (returned, left_updated, right_updated)
        )

    with jax.named_scope("update"):
        update = pl.pallas_call(
            update_kernel,
            out_shape=jax.ShapeDtypeStruct(gradient.shape, gradient.dtype),
            in_specs=[SMEM, VMEM],
            out_specs=VMEM,
            compiler_params=LIMIT,
            cost_estimate=cost(0, 2**20),
        )(part, returned)
    return (left_updated, right_updated, update)


def solution(mesh):
    placed = (
        P(None, "tensor", "fsdp"),
        P(),
        P("fsdp", "tensor", None),
        P("fsdp", "tensor", None),
        P("fsdp", "tensor", None),
        P("fsdp", "tensor", None),
    )
    return jax.shard_map(
        per_device,
        mesh=mesh,
        in_specs=placed,
        out_specs=(P("fsdp", "tensor", None), P("fsdp", "tensor", None), P(None, "tensor", "fsdp")),
        check_vma=False,
    )
```

```python
import functools
import jax
import jax.numpy as jnp
from jax import lax
from jax.experimental import pallas as pl
from jax.experimental.pallas import tpu as pltpu
from jax.sharding import PartitionSpec as P

BETA = 0.999
STEP = 0.5
EPS = 1e-06
TAIL = 16
ROWS = 16
LANES = 128
CORES = 2
VMEM = pl.BlockSpec(memory_space=pltpu.VMEM)
ANY = pl.BlockSpec(memory_space=pl.ANY)
SMEM = pl.BlockSpec(memory_space=pltpu.SMEM)
LIMIT = pltpu.CompilerParams(vmem_limit_bytes=24 * 2**20)


def cost(flops, moved):
    return pl.CostEstimate(flops=flops, bytes_accessed=moved, transcendentals=0)


def slot_numbers(owners_flat):
    total = owners_flat.shape[0]
    same = owners_flat[:, None] == owners_flat[None, :]
    earlier = jnp.arange(total)[None, :] < jnp.arange(total)[:, None]
    return jnp.sum(jnp.where(same & earlier, 1, 0), axis=1).astype(jnp.int32)


def exchange(pieces):
    return lax.all_to_all(pieces, "tensor", split_axis=0, concat_axis=0, tiled=True)


def tile_of(number):
    return pl.ds(number // 2 * ROWS, ROWS), pl.ds(number % 2 * LANES, LANES)


def spread_kernel(part_ref, gradient_ref, out_ref):
    count = gradient_ref.shape[0]
    tiles = out_ref.shape[0] // count
    for group in range(count):
        column = lax.rem(group + count - part_ref[0], count)
        for tile in range(tiles):
            rows, lanes = tile_of(tile)
            out_ref[group * tiles + tile] = gradient_ref[column, rows, lanes]


def pick_kernel(index_ref, tiles_ref, out_ref):
    for at in range(out_ref.shape[0]):
        out_ref[at] = tiles_ref[index_ref[at]]


def pick(index, tiles):
    shape = (index.shape[0],) + tiles.shape[1:]
    return pl.pallas_call(
        pick_kernel,
        out_shape=jax.ShapeDtypeStruct(shape, tiles.dtype),
        in_specs=[SMEM, VMEM],
        out_specs=VMEM,
        compiler_params=LIMIT,
        cost_estimate=cost(0, 2**20),
    )(index, tiles)


def held_rows_kernel(column_ref, used_ref, tiles_ref, sent_ref, rows_ref, sems):
    capacity, _, block_side = rows_ref.shape
    places = sent_ref.shape[0]
    parts = places // (capacity + 1)
    width = block_side // parts
    tiles = tiles_ref.shape[0] // parts
    copies = []
    for slot in range(capacity + 1):
        if slot < capacity:
            keep = used_ref[slot] > 0
            for part in range(parts):
                group = lax.rem(column_ref[slot] + part, parts)
                for tile in range(tiles):
                    rows, lanes = tile_of(tile)
                    lanes = pl.ds(part * width + lanes.start, LANES)
                    value = tiles_ref[group * tiles + tile, slot]
                    rows_ref[slot, rows, lanes] = jnp.where(keep, value, jnp.zeros_like(value))
        for member in range(parts):
            place = slot * parts + member
            source = rows_ref.at[min(slot, capacity - 1)]
            copies.append(pltpu.make_async_copy(source, sent_ref.at[place], sems.at[place]))
            copies[-1].start()
    for copy in copies:
        copy.wait()


def held_rows(column_of, used, tiles, height, block_side, places):
    capacity = tiles.shape[1]
    return pl.pallas_call(
        held_rows_kernel,
        out_shape=jax.ShapeDtypeStruct((places, height, block_side), tiles.dtype),
        in_specs=[SMEM, SMEM, VMEM],
        out_specs=ANY,
        scratch_shapes=[
            pltpu.VMEM((capacity, height, block_side), tiles.dtype),
            pltpu.SemaphoreType.DMA((places,)),
        ],
        compiler_params=LIMIT,
        cost_estimate=cost(0, 4 * 2**20),
    )(column_of, used, tiles)


def three_parts(value):
    high = value.astype(jnp.bfloat16)
    rest = value - high.astype(jnp.float32)
    middle = rest.astype(jnp.bfloat16)
    return [high, middle, (rest - middle.astype(jnp.float32)).astype(jnp.bfloat16)]


def around(place, step, count):
    return lax.rem(place + count - step, count)


def precondition_kernel(side, origins, place_ref, *refs):
    left_ref, right_ref, block_ref, out_ref = refs
    y, x = place_ref[0], place_ref[1]
    places, height, block_side = block_ref.shape
    width = block_side // side
    cores = out_ref.shape[0] // places
    narrow = width // side
    block = block_ref[...].reshape(block_side, block_side)
    right = jnp.concatenate([right_ref[around(y, at, side)] for at in range(side)], axis=0)
    power = jnp.zeros((1, width), jnp.float32)
    for begin in range(0, places, side):
        left = left_ref[pl.ds(begin, side)].reshape(side * height, block_side)
        mixed = jnp.dot(left, block, preferred_element_type=jnp.float32).astype(jnp.bfloat16)
        product = lax.dot_general(
            mixed, right, (((1,), (1,)), ((), ())), preferred_element_type=jnp.float32
        )
        power += jnp.sum(product * product, axis=0, keepdims=True)
        product = product.astype(jnp.bfloat16)
        for core in range(cores):
            share = jnp.concatenate(
                [
                    product[:, part * narrow : (part + 1) * narrow]
                    for part in range(core, side, cores)
                ],
                axis=1,
            )
            for at, (row, column) in enumerate(origins[begin : begin + side]):
                place = core * places + around(y, row, side) * side + around(x, column, side)
                out_ref[place, pl.ds(0, height), :] = share[at * height : (at + 1) * height]
    share = places // side
    own = block_ref[pl.ds(x * share, share)].astype(jnp.float32).reshape(width, block_side)
    own = jnp.sum(own * own, axis=0, keepdims=True)
    grad = sum(own[:, at : at + LANES] for at in range(0, block_side, LANES))
    power = sum(power[:, at : at + LANES] for at in range(0, width, LANES))
    number = lax.broadcasted_iota(jnp.int32, (TAIL, LANES), 0)
    tail = jnp.zeros((TAIL, LANES), jnp.float32)
    for at, line in enumerate(three_parts(power) + three_parts(grad)):
        tail = jnp.where(number == at, line.astype(jnp.float32), tail)
    tail = tail.astype(jnp.bfloat16)
    for place in range(places * cores):
        out_ref[place, pl.ds(height, TAIL), :] = tail


def precondition(place, left, origins, right, block):
    places, height, block_side = block.shape
    side = right.shape[0]
    width = block_side // side
    return pl.pallas_call(
        functools.partial(precondition_kernel, side, origins),
        out_shape=jax.ShapeDtypeStruct((places * CORES, height + TAIL, LANES), jnp.bfloat16),
        in_specs=[SMEM] + [VMEM] * 3,
        out_specs=VMEM,
        compiler_params=pltpu.CompilerParams(vmem_limit_bytes=32 * 2**20),
        cost_estimate=cost(2 * block_side * block_side * (block_side + width), 6 * 2**20),
    )(place, left, right, block)


def steps_kernel(side, column_ref, back_ref, out_ref):
    height = back_ref.shape[1] - TAIL
    tiles = out_ref.shape[0] // CORES
    narrow = back_ref.shape[2] // CORES
    slots = column_ref.shape[0]
    for held in range(slots):
        core, slot = held // (slots // CORES), held % (slots // CORES)
        first = core * (back_ref.shape[0] // CORES) + slot * side
        sums = sum(
            back_ref[first + member, pl.ds(height, TAIL), :].astype(jnp.float32)
            for member in range(side)
        )
        sums = jnp.sum(sums, axis=1, keepdims=True)
        power = jnp.sum(sums[0:3], axis=0, keepdims=True)
        grad = jnp.sum(sums[3:6], axis=0, keepdims=True)
        scale = -STEP * jnp.sqrt(grad) * lax.rsqrt(power + EPS)
        rows_of = [
            (scale * back_ref[first + member, pl.ds(0, height), :].astype(jnp.float32)).astype(
                jnp.bfloat16
            )
            for member in range(side)
        ]
        for half in range(CORES):
            group = lax.rem(column_ref[held] + half, CORES)
            chunk = jnp.concatenate(
                [rows[:, half * narrow : (half + 1) * narrow] for rows in rows_of], axis=1
            )
            for tile in range(tiles):
                rows, lanes = tile_of(tile)
                out_ref[group * tiles + tile, held] = chunk[
                    rows.start : rows.start + ROWS, lanes.start : lanes.start + LANES
                ]


def update_kernel(half_ref, tiles_ref, out_ref):
    tiles = tiles_ref.shape[0] // CORES
    for column in range(out_ref.shape[0]):
        group = lax.rem(column + half_ref[0], CORES)
        for tile in range(tiles):
            rows, lanes = tile_of(tile)
            out_ref[column, rows, lanes] = tiles_ref[group * tiles + tile, column // CORES]


def statistics_kernel(side, place_ref, left_ref, right_ref, *refs):
    term_refs, outs = refs[:side], refs[side:]
    for step in range(side):
        slot = around(place_ref[0], step, side)

        @pl.when(slot < left_ref.shape[0])
        def _():
            for kind, (old, new) in enumerate(zip((left_ref, right_ref), outs)):
                term = term_refs[step][kind].astype(jnp.float32)
                new[slot] = BETA * old[slot] + (1.0 - BETA) * term


def per_device(gradient, block_owner, left_stats, right_stats, left_root, right_root):
    tensor_index = lax.axis_index("tensor")
    fsdp_index = lax.axis_index("fsdp")
    fsdp_count = lax.axis_size("fsdp")
    tensor_count = lax.axis_size("tensor")
    col_blocks, local_height, row_depth = gradient.shape
    row_blocks = block_owner.shape[1]
    capacity, _, block_side = left_stats.shape
    side = block_side // row_depth
    y, x = tensor_index // side, tensor_index % side
    place = jnp.stack([y, x]).astype(jnp.int32)

    def along_y(value, step, sources, targets):
        pairs = [
            (a * side + b, (a + step) % side * side + b)
            for a in range(side)
            for b in range(side)
            if a < sources and (a + step) % side < targets
        ]
        return lax.ppermute(value, "tensor", pairs)

    def along_x(value, step, rows):
        pairs = [
            (a * side + b, a * side + (b + step) % side) for a in range(rows) for b in range(side)
        ]
        return lax.ppermute(value, "tensor", pairs)

    def over_rows(value):
        return lax.all_to_all(value, "fsdp", split_axis=0, concat_axis=0, tiled=True)

    chips = fsdp_count // CORES

    def along_z(value):
        rings = [[chip * CORES + core for chip in range(chips)] for core in range(CORES)]
        return lax.all_to_all(
            value, "fsdp", split_axis=0, concat_axis=0, tiled=True, axis_index_groups=rings
        )

    def over_chip_planes(value):
        count = CORES * tensor_count
        planes = [[chip * count + member for member in range(count)] for chip in range(chips)]
        return lax.all_to_all(
            value,
            ("fsdp", "tensor"),
            split_axis=0,
            concat_axis=0,
            tiled=True,
            axis_index_groups=planes,
        )

    part = (fsdp_index % side).astype(jnp.int32).reshape(1)
    group = fsdp_index // (fsdp_count // col_blocks)

    with jax.named_scope("gradient_spread"):
        spread = pl.pallas_call(
            spread_kernel,
            out_shape=jax.ShapeDtypeStruct((fsdp_count, ROWS, LANES), gradient.dtype),
            in_specs=[SMEM, VMEM],
            out_specs=VMEM,
            compiler_params=LIMIT,
            cost_estimate=cost(0, 2**18),
        )(part, gradient)
        spread, left_root, right_root = lax.optimization_barrier((spread, left_root, right_root))
        spread = over_rows(spread)

    with jax.named_scope("where_blocks_go"):
        owners_flat = block_owner.reshape(-1)
        numbers = jnp.arange(owners_flat.shape[0])
        column_flat, band_flat = numbers // row_blocks, numbers % row_blocks
        entries = owners_flat * capacity + slot_numbers(owners_flat)
        held_at = entries[:, None] == jnp.arange(fsdp_count * capacity)[None, :]
        source = band_flat * side + (group - column_flat + side) % side
        forward = jnp.sum(jnp.where(held_at, source[:, None], 0), axis=0).astype(jnp.int32)
        mine = entries[:, None] == (fsdp_index * capacity + jnp.arange(capacity))[None, :]
        used = jnp.any(mine, axis=0).astype(jnp.int32)
        column_of = jnp.sum(jnp.where(mine, column_flat[:, None], 0), axis=0).astype(jnp.int32)
        chip = fsdp_index // CORES
        ours = (chip * CORES * capacity + jnp.arange(CORES * capacity))[None, :]
        columns_here = jnp.sum(
            jnp.where(entries[:, None] == ours, column_flat[:, None], 0), axis=0
        ).astype(jnp.int32)
        homes = jnp.arange(chips)[:, None]
        turn = (chip // (chips // CORES) - homes % CORES + CORES) % CORES
        wanted = CORES * jnp.arange(col_blocks // CORES)[None, :] + turn
        wanted = (wanted * row_blocks + homes // CORES).reshape(-1)
        backward = jnp.sum(
            jnp.where(wanted[:, None] == numbers[None, :], entries[None, :], 0), axis=1
        ).astype(jnp.int32)
        half_here = (chip % CORES).astype(jnp.int32).reshape(1)

    with jax.named_scope("gradient_to_owners"):
        sent = pick(forward, spread).reshape(fsdp_count, capacity, ROWS, LANES)
        tiles = over_rows(sent)

    with jax.named_scope("roots_to_slot_groups"):
        roots = jnp.stack([left_root, right_root], axis=1)
        taken = []
        for step in range(side):
            slot = jnp.minimum((y + step) % side, capacity - 1)
            own = lax.dynamic_index_in_dim(roots, slot, 0, keepdims=False)
            taken.append(along_y(own, step, side, capacity) if step else own)
        left_rows = jnp.stack([piece[0] for piece in taken])
        right_rows = jnp.stack([piece[1] for piece in taken])
        half = side // 2
        before = along_x(left_rows, 1, capacity)
        behind = along_x(left_rows, side - 1, capacity)
        lefts = [
            left_rows,
            before,
            behind,
            along_x(before[:half], 1, capacity),
            along_x(behind[half:], side - 1, capacity),
        ]
        origins = [
            (row, column) for column in (0, 1, side - 1, half) for row in range(side)
        ]
        tiles, right_rows, *lefts = lax.optimization_barrier((tiles, right_rows, *lefts))

    with jax.named_scope("rows_of_held_blocks"):
        sent = held_rows(column_of, used, tiles, local_height, block_side, tensor_count)
        sent, *lefts = lax.optimization_barrier((sent, *lefts))
        block = exchange(sent)
        left = jnp.concatenate(lefts)

    with jax.named_scope("precondition"):
        leaving = precondition(place, left, origins, right_rows, block)

    with jax.named_scope("step_to_gradient_rows"):
        back = over_chip_planes(leaving)
        block, leaving = lax.optimization_barrier((block, leaving))
        block = block.reshape(block_side, block_side)
        own_rows = lax.dynamic_index_in_dim(
            block.reshape(side, side, local_height, block_side), x, 1, keepdims=False
        ).reshape(row_depth, block_side)
        own_columns = jnp.concatenate(
            [
                lax.dynamic_slice_in_dim(block, (at * side + x) * local_height, local_height, 1)
                for at in range(side)
            ],
            axis=1,
        )
        left_term = jnp.einsum("ak,jk->aj", own_rows, block, preferred_element_type=jnp.float32)
        right_term = jnp.einsum("ja,jk->ak", own_columns, block, preferred_element_type=jnp.float32)
        terms = jnp.stack([left_term.astype(jnp.bfloat16), right_term.astype(jnp.bfloat16)])
        terms = terms.reshape(2, side, local_height, block_side)
        terms = [
            lax.dynamic_index_in_dim(terms, (y + step) % side, 1, keepdims=False)
            for step in range(side)
        ]
        back, *terms = lax.optimization_barrier((back, *terms))
        steps = pl.pallas_call(
            functools.partial(steps_kernel, side),
            out_shape=jax.ShapeDtypeStruct((chips, CORES * capacity, ROWS, LANES), jnp.bfloat16),
            in_specs=[SMEM, VMEM],
            out_specs=VMEM,
            compiler_params=LIMIT,
            cost_estimate=cost(0, 2 * 2**20),
        )(columns_here, back)
        steps, *terms = lax.optimization_barrier((steps, *terms))
        passing = along_z(steps).reshape(fsdp_count * capacity, ROWS, LANES)

    with jax.named_scope("statistics"):
        arrived = terms[:1] + [
            along_y(terms[step], step, capacity, side) for step in range(1, side)
        ]
        passing, *arrived = lax.optimization_barrier((passing, *arrived))
        returned = along_z(
            pick(backward, passing).reshape(chips, col_blocks // CORES, ROWS, LANES)
        )
        left_updated, right_updated = pl.pallas_call(
            functools.partial(statistics_kernel, side),
            out_shape=(
                jax.ShapeDtypeStruct(left_stats.shape, left_stats.dtype),
                jax.ShapeDtypeStruct(right_stats.shape, right_stats.dtype),
            ),
            in_specs=[SMEM] + [VMEM] * (2 + side),
            out_specs=(VMEM, VMEM),
            compiler_params=LIMIT,
            cost_estimate=cost(0, 4 * 2**20),
        )(place, left_stats, right_stats, *arrived)
        returned, left_updated, right_updated = lax.optimization_barrier(
            (returned, left_updated, right_updated)
        )

    with jax.named_scope("update"):
        update = pl.pallas_call(
            update_kernel,
            out_shape=jax.ShapeDtypeStruct(gradient.shape, gradient.dtype),
            in_specs=[SMEM, VMEM],
            out_specs=VMEM,
            compiler_params=LIMIT,
            cost_estimate=cost(0, 2**20),
        )(half_here, returned)
    return (left_updated, right_updated, update)


def solution(mesh):
    placed = (
        P(None, "tensor", "fsdp"),
        P(),
        P("fsdp", "tensor", None),
        P("fsdp", "tensor", None),
        P("fsdp", "tensor", None),
        P("fsdp", "tensor", None),
    )
    return jax.shard_map(
        per_device,
        mesh=mesh,
        in_specs=placed,
        out_specs=(P("fsdp", "tensor", None), P("fsdp", "tensor", None), P(None, "tensor", "fsdp")),
        check_vma=False,
    )
```

```python
import functools
import jax
import jax.numpy as jnp
from jax import lax
from jax.experimental import pallas as pl
from jax.experimental.pallas import tpu as pltpu
from jax.sharding import PartitionSpec as P

BETA = 0.999
STEP = 0.5
EPS = 1e-06
TAIL = 16
ROWS = 16
LANES = 128
CORES = 2
VMEM = pl.BlockSpec(memory_space=pltpu.VMEM)
ANY = pl.BlockSpec(memory_space=pl.ANY)
SMEM = pl.BlockSpec(memory_space=pltpu.SMEM)
LIMIT = pltpu.CompilerParams(vmem_limit_bytes=24 * 2**20)


def cost(flops, moved):
    return pl.CostEstimate(flops=flops, bytes_accessed=moved, transcendentals=0)


def slot_numbers(owners_flat):
    total = owners_flat.shape[0]
    same = owners_flat[:, None] == owners_flat[None, :]
    earlier = jnp.arange(total)[None, :] < jnp.arange(total)[:, None]
    return jnp.sum(jnp.where(same & earlier, 1, 0), axis=1).astype(jnp.int32)


def exchange(pieces):
    return lax.all_to_all(pieces, "tensor", split_axis=0, concat_axis=0, tiled=True)


def tile_of(number):
    return pl.ds(number // 2 * ROWS, ROWS), pl.ds(number % 2 * LANES, LANES)


def spread_kernel(part_ref, gradient_ref, out_ref):
    count = gradient_ref.shape[0]
    tiles = out_ref.shape[0] // count
    for group in range(count):
        column = lax.rem(group + count - part_ref[0], count)
        for tile in range(tiles):
            rows, lanes = tile_of(tile)
            out_ref[group * tiles + tile] = gradient_ref[column, rows, lanes]


def pick_kernel(index_ref, tiles_ref, out_ref):
    for at in range(out_ref.shape[0]):
        out_ref[at] = tiles_ref[index_ref[at]]


def pick(index, tiles):
    shape = (index.shape[0],) + tiles.shape[1:]
    return pl.pallas_call(
        pick_kernel,
        out_shape=jax.ShapeDtypeStruct(shape, tiles.dtype),
        in_specs=[SMEM, VMEM],
        out_specs=VMEM,
        compiler_params=LIMIT,
        cost_estimate=cost(0, 2**20),
    )(index, tiles)


def held_rows_kernel(column_ref, used_ref, tiles_ref, sent_ref, rows_ref, sems):
    capacity, _, block_side = rows_ref.shape
    places = sent_ref.shape[0]
    parts = places // (capacity + 1)
    width = block_side // parts
    tiles = tiles_ref.shape[0] // parts
    copies = []
    for slot in range(capacity + 1):
        if slot < capacity:
            keep = used_ref[slot] > 0
            for part in range(parts):
                group = lax.rem(column_ref[slot] + part, parts)
                for tile in range(tiles):
                    rows, lanes = tile_of(tile)
                    lanes = pl.ds(part * width + lanes.start, LANES)
                    value = tiles_ref[group * tiles + tile, slot]
                    rows_ref[slot, rows, lanes] = jnp.where(keep, value, jnp.zeros_like(value))
        for member in range(parts):
            place = slot * parts + member
            source = rows_ref.at[min(slot, capacity - 1)]
            copies.append(pltpu.make_async_copy(source, sent_ref.at[place], sems.at[place]))
            copies[-1].start()
    for copy in copies:
        copy.wait()


def held_rows(column_of, used, tiles, height, block_side, places):
    capacity = tiles.shape[1]
    return pl.pallas_call(
        held_rows_kernel,
        out_shape=jax.ShapeDtypeStruct((places, height, block_side), tiles.dtype),
        in_specs=[SMEM, SMEM, VMEM],
        out_specs=ANY,
        scratch_shapes=[
            pltpu.VMEM((capacity, height, block_side), tiles.dtype),
            pltpu.SemaphoreType.DMA((places,)),
        ],
        compiler_params=LIMIT,
        cost_estimate=cost(0, 4 * 2**20),
    )(column_of, used, tiles)


def three_parts(value):
    high = value.astype(jnp.bfloat16)
    rest = value - high.astype(jnp.float32)
    middle = rest.astype(jnp.bfloat16)
    return [high, middle, (rest - middle.astype(jnp.float32)).astype(jnp.bfloat16)]


def around(place, step, count):
    return lax.rem(place + count - step, count)


def turn_kernel(side, place_ref, root_ref, out_ref):
    x = place_ref[1]
    block_side = root_ref.shape[2]
    width, narrow = block_side // side, block_side // side // side
    for slot in range(root_ref.shape[0]):
        for column in range(side):
            chunk = [
                root_ref[slot, :, pl.ds(row * width + column * narrow, narrow)]
                for row in range(side)
            ]
            lanes = pl.ds(pl.multiple_of(around(column, x, side) * width, width), width)
            out_ref[slot, :, lanes] = jnp.concatenate(chunk, axis=1)


def whole_root_kernel(side, place_ref, own_ref, before_ref, behind_ref, far_ref, out_ref, turned_ref):
    y, x = place_ref[0], place_ref[1]
    block_side = own_ref.shape[2]
    width, narrow = block_side // side, block_side // side // side

    def block(ref, number):
        return jnp.concatenate(
            [
                ref[around(y, at, side), :, pl.ds(number * width, width)]
                for at in range(side)
            ],
            axis=0,
        )

    given = {(0, 0): block(own_ref, 0)}
    for number in range(1, side):
        given[0, number] = block(own_ref, number)
    given[3, 3], given[3, 1], given[3, 2] = (block(before_ref, number) for number in range(3))
    given[1, 1], given[1, 2] = (block(behind_ref, number) for number in range(2))
    given[2, 2] = block(far_ref, 0)
    for first in range(side):
        for second in range(side):
            if (first, second) in given:
                value = given[first, second]
            else:
                value = given[second, first].astype(jnp.float32).T.astype(own_ref.dtype)
            turned_ref[pl.ds(first * width, width), pl.ds(second * width, width)] = value
    for first in range(side):
        rows = pl.ds(first * width, width)
        for column in range(side):
            lanes = pl.ds(pl.multiple_of(around(column, x, side) * width, width), width)
            chunk = turned_ref[rows, lanes]
            for row in range(side):
                out_ref[rows, pl.ds(row * width + column * narrow, narrow)] = chunk[
                    :, row * narrow : (row + 1) * narrow
                ]


def precondition_kernel(side, place_ref, left_ref, right_ref, block_ref, out_ref):
    y, x = place_ref[0], place_ref[1]
    places, height, block_side = block_ref.shape
    width = block_side // side
    cores = out_ref.shape[0] // places
    narrow = width // side
    block = block_ref[...].reshape(block_side, block_side)
    right = jnp.concatenate([right_ref[around(y, at, side)] for at in range(side)], axis=0)
    power = jnp.zeros((1, width), jnp.float32)
    for begin in range(0, places, side):
        left = left_ref[pl.ds(begin, side)].reshape(side * height, block_side)
        mixed = jnp.dot(left, block, preferred_element_type=jnp.float32).astype(jnp.bfloat16)
        product = lax.dot_general(
            mixed, right, (((1,), (1,)), ((), ())), preferred_element_type=jnp.float32
        )
        power += jnp.sum(product * product, axis=0, keepdims=True)
        product = product.astype(jnp.bfloat16)
        for core in range(cores):
            share = jnp.concatenate(
                [
                    product[:, part * narrow : (part + 1) * narrow]
                    for part in range(core, side, cores)
                ],
                axis=1,
            )
            for at in range(side):
                place = core * places + at * side + lax.rem(x + begin // side, side)
                out_ref[place, pl.ds(0, height), :] = share[at * height : (at + 1) * height]
    share = places // side
    own = block_ref[pl.ds(x * share, share)].astype(jnp.float32).reshape(width, block_side)
    own = jnp.sum(own * own, axis=0, keepdims=True)
    grad = sum(own[:, at : at + LANES] for at in range(0, block_side, LANES))
    power = sum(power[:, at : at + LANES] for at in range(0, width, LANES))
    number = lax.broadcasted_iota(jnp.int32, (TAIL, LANES), 0)
    tail = jnp.zeros((TAIL, LANES), jnp.float32)
    for at, line in enumerate(three_parts(power) + three_parts(grad)):
        tail = jnp.where(number == at, line.astype(jnp.float32), tail)
    tail = tail.astype(jnp.bfloat16)
    for place in range(places * cores):
        out_ref[place, pl.ds(height, TAIL), :] = tail


def precondition(place, left, right, block):
    places, height, block_side = block.shape
    side = right.shape[0]
    width = block_side // side
    return pl.pallas_call(
        functools.partial(precondition_kernel, side),
        out_shape=jax.ShapeDtypeStruct((places * CORES, height + TAIL, LANES), jnp.bfloat16),
        in_specs=[SMEM] + [VMEM] * 3,
        out_specs=VMEM,
        compiler_params=pltpu.CompilerParams(vmem_limit_bytes=32 * 2**20),
        cost_estimate=cost(2 * block_side * block_side * (block_side + width), 6 * 2**20),
    )(place, left, right, block)


def steps_kernel(side, column_ref, back_ref, out_ref):
    height = back_ref.shape[1] - TAIL
    tiles = out_ref.shape[0] // CORES
    narrow = back_ref.shape[2] // CORES
    slots = column_ref.shape[0]
    for held in range(slots):
        core, slot = held // (slots // CORES), held % (slots // CORES)
        first = core * (back_ref.shape[0] // CORES) + slot * side
        sums = sum(
            back_ref[first + member, pl.ds(height, TAIL), :].astype(jnp.float32)
            for member in range(side)
        )
        sums = jnp.sum(sums, axis=1, keepdims=True)
        power = jnp.sum(sums[0:3], axis=0, keepdims=True)
        grad = jnp.sum(sums[3:6], axis=0, keepdims=True)
        scale = -STEP * jnp.sqrt(grad) * lax.rsqrt(power + EPS)
        rows_of = [
            (scale * back_ref[first + member, pl.ds(0, height), :].astype(jnp.float32)).astype(
                jnp.bfloat16
            )
            for member in range(side)
        ]
        for half in range(CORES):
            group = lax.rem(column_ref[held] + half, CORES)
            chunk = jnp.concatenate(
                [rows[:, half * narrow : (half + 1) * narrow] for rows in rows_of], axis=1
            )
            for tile in range(tiles):
                rows, lanes = tile_of(tile)
                out_ref[group * tiles + tile, held] = chunk[
                    rows.start : rows.start + ROWS, lanes.start : lanes.start + LANES
                ]


def update_kernel(half_ref, tiles_ref, out_ref):
    tiles = tiles_ref.shape[0] // CORES
    for column in range(out_ref.shape[0]):
        group = lax.rem(column + half_ref[0], CORES)
        for tile in range(tiles):
            rows, lanes = tile_of(tile)
            out_ref[column, rows, lanes] = tiles_ref[group * tiles + tile, column // CORES]


def statistics_kernel(side, place_ref, left_ref, right_ref, *refs):
    term_refs, outs = refs[:side], refs[side:]
    for step in range(side):
        slot = around(place_ref[0], step, side)

        @pl.when(slot < left_ref.shape[0])
        def _():
            for kind, (old, new) in enumerate(zip((left_ref, right_ref), outs)):
                term = term_refs[step][kind].astype(jnp.float32)
                new[slot] = BETA * old[slot] + (1.0 - BETA) * term


def per_device(gradient, block_owner, left_stats, right_stats, left_root, right_root):
    tensor_index = lax.axis_index("tensor")
    fsdp_index = lax.axis_index("fsdp")
    fsdp_count = lax.axis_size("fsdp")
    tensor_count = lax.axis_size("tensor")
    col_blocks, local_height, row_depth = gradient.shape
    row_blocks = block_owner.shape[1]
    capacity, _, block_side = left_stats.shape
    side = block_side // row_depth
    y, x = tensor_index // side, tensor_index % side
    place = jnp.stack([y, x]).astype(jnp.int32)

    def along_y(value, step, sources, targets):
        pairs = [
            (a * side + b, (a + step) % side * side + b)
            for a in range(side)
            for b in range(side)
            if a < sources and (a + step) % side < targets
        ]
        return lax.ppermute(value, "tensor", pairs)

    def along_x(value, step, rows):
        pairs = [
            (a * side + b, a * side + (b + step) % side) for a in range(rows) for b in range(side)
        ]
        return lax.ppermute(value, "tensor", pairs)

    def over_rows(value):
        return lax.all_to_all(value, "fsdp", split_axis=0, concat_axis=0, tiled=True)

    chips = fsdp_count // CORES

    def along_z(value):
        rings = [[chip * CORES + core for chip in range(chips)] for core in range(CORES)]
        return lax.all_to_all(
            value, "fsdp", split_axis=0, concat_axis=0, tiled=True, axis_index_groups=rings
        )

    def over_chip_planes(value):
        count = CORES * tensor_count
        planes = [[chip * count + member for member in range(count)] for chip in range(chips)]
        return lax.all_to_all(
            value,
            ("fsdp", "tensor"),
            split_axis=0,
            concat_axis=0,
            tiled=True,
            axis_index_groups=planes,
        )

    part = (fsdp_index % side).astype(jnp.int32).reshape(1)
    group = fsdp_index // (fsdp_count // col_blocks)

    with jax.named_scope("gradient_spread"):
        spread = pl.pallas_call(
            spread_kernel,
            out_shape=jax.ShapeDtypeStruct((fsdp_count, ROWS, LANES), gradient.dtype),
            in_specs=[SMEM, VMEM],
            out_specs=VMEM,
            compiler_params=LIMIT,
            cost_estimate=cost(0, 2**18),
        )(part, gradient)
        spread, left_root, right_root = lax.optimization_barrier((spread, left_root, right_root))
        spread = over_rows(spread)

    with jax.named_scope("where_blocks_go"):
        owners_flat = block_owner.reshape(-1)
        numbers = jnp.arange(owners_flat.shape[0])
        column_flat, band_flat = numbers // row_blocks, numbers % row_blocks
        entries = owners_flat * capacity + slot_numbers(owners_flat)
        held_at = entries[:, None] == jnp.arange(fsdp_count * capacity)[None, :]
        source = band_flat * side + (group - column_flat + side) % side
        forward = jnp.sum(jnp.where(held_at, source[:, None], 0), axis=0).astype(jnp.int32)
        mine = entries[:, None] == (fsdp_index * capacity + jnp.arange(capacity))[None, :]
        used = jnp.any(mine, axis=0).astype(jnp.int32)
        column_of = jnp.sum(jnp.where(mine, column_flat[:, None], 0), axis=0).astype(jnp.int32)
        chip = fsdp_index // CORES
        ours = (chip * CORES * capacity + jnp.arange(CORES * capacity))[None, :]
        columns_here = jnp.sum(
            jnp.where(entries[:, None] == ours, column_flat[:, None], 0), axis=0
        ).astype(jnp.int32)
        homes = jnp.arange(chips)[:, None]
        turn = (chip // (chips // CORES) - homes % CORES + CORES) % CORES
        wanted = CORES * jnp.arange(col_blocks // CORES)[None, :] + turn
        wanted = (wanted * row_blocks + homes // CORES).reshape(-1)
        backward = jnp.sum(
            jnp.where(wanted[:, None] == numbers[None, :], entries[None, :], 0), axis=1
        ).astype(jnp.int32)
        half_here = (chip % CORES).astype(jnp.int32).reshape(1)

    with jax.named_scope("gradient_to_owners"):
        sent = pick(forward, spread).reshape(fsdp_count, capacity, ROWS, LANES)
        tiles = over_rows(sent)

    with jax.named_scope("roots_to_slot_groups"):
        turned = pl.pallas_call(
            functools.partial(turn_kernel, side),
            out_shape=jax.ShapeDtypeStruct(left_root.shape, left_root.dtype),
            in_specs=[SMEM, VMEM],
            out_specs=VMEM,
            compiler_params=LIMIT,
            cost_estimate=cost(0, 2**20),
        )(place, left_root)
        roots = jnp.stack([turned, right_root], axis=1)
        taken = []
        for step in range(side):
            slot = jnp.minimum((y + step) % side, capacity - 1)
            own = lax.dynamic_index_in_dim(roots, slot, 0, keepdims=False)
            taken.append(along_y(own, step, side, capacity) if step else own)
        left_rows = jnp.stack([piece[0] for piece in taken])
        right_rows = jnp.stack([piece[1] for piece in taken])
        width = row_depth
        lefts = [
            left_rows,
            along_x(
                jnp.concatenate([left_rows[:, :, :width], left_rows[:, :, 2 * width :]], axis=2),
                1,
                capacity,
            ),
            along_x(left_rows[:, :, : 2 * width], side - 1, capacity),
            along_x(left_rows[:, :, :width], 2, capacity),
        ]
        tiles, right_rows, *lefts = lax.optimization_barrier((tiles, right_rows, *lefts))

    with jax.named_scope("rows_of_held_blocks"):
        sent = held_rows(column_of, used, tiles, local_height, block_side, tensor_count)
        sent, *lefts = lax.optimization_barrier((sent, *lefts))
        block = exchange(sent)
        left = pl.pallas_call(
            functools.partial(whole_root_kernel, side),
            out_shape=jax.ShapeDtypeStruct((block_side, block_side), left_root.dtype),
            in_specs=[SMEM] + [VMEM] * len(lefts),
            out_specs=VMEM,
            scratch_shapes=[pltpu.VMEM((block_side, block_side), left_root.dtype)],
            compiler_params=LIMIT,
            cost_estimate=cost(0, 8 * 2**20),
        )(place, *lefts)
        left = left.reshape(tensor_count, local_height, block_side)

    with jax.named_scope("precondition"):
        leaving = precondition(place, left, right_rows, block)

    with jax.named_scope("step_to_gradient_rows"):
        back = over_chip_planes(leaving)
        block, leaving = lax.optimization_barrier((block, leaving))
        block = block.reshape(block_side, block_side)
        own_rows = lax.dynamic_index_in_dim(
            block.reshape(side, side, local_height, block_side), x, 1, keepdims=False
        ).reshape(row_depth, block_side)
        own_columns = jnp.concatenate(
            [
                lax.dynamic_slice_in_dim(block, (at * side + x) * local_height, local_height, 1)
                for at in range(side)
            ],
            axis=1,
        )
        left_term = jnp.einsum("ak,jk->aj", own_rows, block, preferred_element_type=jnp.float32)
        right_term = jnp.einsum("ja,jk->ak", own_columns, block, preferred_element_type=jnp.float32)
        terms = jnp.stack([left_term.astype(jnp.bfloat16), right_term.astype(jnp.bfloat16)])
        terms = terms.reshape(2, side, local_height, block_side)
        terms = [
            lax.dynamic_index_in_dim(terms, (y + step) % side, 1, keepdims=False)
            for step in range(side)
        ]
        back, *terms = lax.optimization_barrier((back, *terms))
        steps = pl.pallas_call(
            functools.partial(steps_kernel, side),
            out_shape=jax.ShapeDtypeStruct((chips, CORES * capacity, ROWS, LANES), jnp.bfloat16),
            in_specs=[SMEM, VMEM],
            out_specs=VMEM,
            compiler_params=LIMIT,
            cost_estimate=cost(0, 2 * 2**20),
        )(columns_here, back)
        steps, *terms = lax.optimization_barrier((steps, *terms))
        passing = along_z(steps).reshape(fsdp_count * capacity, ROWS, LANES)

    with jax.named_scope("statistics"):
        arrived = terms[:1] + [
            along_y(terms[step], step, capacity, side) for step in range(1, side)
        ]
        passing, *arrived = lax.optimization_barrier((passing, *arrived))
        returned = along_z(
            pick(backward, passing).reshape(chips, col_blocks // CORES, ROWS, LANES)
        )
        left_updated, right_updated = pl.pallas_call(
            functools.partial(statistics_kernel, side),
            out_shape=(
                jax.ShapeDtypeStruct(left_stats.shape, left_stats.dtype),
                jax.ShapeDtypeStruct(right_stats.shape, right_stats.dtype),
            ),
            in_specs=[SMEM] + [VMEM] * (2 + side),
            out_specs=(VMEM, VMEM),
            compiler_params=LIMIT,
            cost_estimate=cost(0, 4 * 2**20),
        )(place, left_stats, right_stats, *arrived)
        returned, left_updated, right_updated = lax.optimization_barrier(
            (returned, left_updated, right_updated)
        )

    with jax.named_scope("update"):
        update = pl.pallas_call(
            update_kernel,
            out_shape=jax.ShapeDtypeStruct(gradient.shape, gradient.dtype),
            in_specs=[SMEM, VMEM],
            out_specs=VMEM,
            compiler_params=LIMIT,
            cost_estimate=cost(0, 2**20),
        )(half_here, returned)
    return (left_updated, right_updated, update)


def solution(mesh):
    placed = (
        P(None, "tensor", "fsdp"),
        P(),
        P("fsdp", "tensor", None),
        P("fsdp", "tensor", None),
        P("fsdp", "tensor", None),
        P("fsdp", "tensor", None),
    )
    return jax.shard_map(
        per_device,
        mesh=mesh,
        in_specs=placed,
        out_specs=(P("fsdp", "tensor", None), P("fsdp", "tensor", None), P(None, "tensor", "fsdp")),
        check_vma=False,
    )
```

```python
import functools
import jax
import jax.numpy as jnp
from jax import lax
from jax.experimental import pallas as pl
from jax.experimental.pallas import tpu as pltpu
from jax.sharding import PartitionSpec as P

BETA = 0.999
STEP = 0.5
EPS = 1e-06
TAIL = 16
ROWS = 16
LANES = 128
CORES = 2
VMEM = pl.BlockSpec(memory_space=pltpu.VMEM)
ANY = pl.BlockSpec(memory_space=pl.ANY)
SMEM = pl.BlockSpec(memory_space=pltpu.SMEM)
LIMIT = pltpu.CompilerParams(vmem_limit_bytes=24 * 2**20)


def cost(flops, moved):
    return pl.CostEstimate(flops=flops, bytes_accessed=moved, transcendentals=0)


def slot_numbers(owners_flat):
    total = owners_flat.shape[0]
    same = owners_flat[:, None] == owners_flat[None, :]
    earlier = jnp.arange(total)[None, :] < jnp.arange(total)[:, None]
    return jnp.sum(jnp.where(same & earlier, 1, 0), axis=1).astype(jnp.int32)


def tile_of(number):
    return pl.ds(number // 2 * ROWS, ROWS), pl.ds(number % 2 * LANES, LANES)


def spread_kernel(half_ref, gradient_ref, out_ref):
    tiles = out_ref.shape[0] // CORES
    for group in range(CORES):
        for pair in range(out_ref.shape[1]):
            column = CORES * pair + lax.rem(group + CORES - half_ref[0], CORES)
            for tile in range(tiles):
                rows, lanes = tile_of(tile)
                out_ref[group * tiles + tile, pair] = gradient_ref[column, rows, lanes]


def pick_kernel(index_ref, tiles_ref, out_ref):
    for at in range(out_ref.shape[0]):
        out_ref[at] = tiles_ref[index_ref[at]]


def pick(index, tiles):
    shape = (index.shape[0],) + tiles.shape[1:]
    return pl.pallas_call(
        pick_kernel,
        out_shape=jax.ShapeDtypeStruct(shape, tiles.dtype),
        in_specs=[SMEM, VMEM],
        out_specs=VMEM,
        compiler_params=LIMIT,
        cost_estimate=cost(0, 2**20),
    )(index, tiles)


def held_rows_kernel(column_ref, used_ref, tiles_ref, sent_ref, rows_ref, sems):
    capacity = rows_ref.shape[0] // CORES
    width = rows_ref.shape[2] // CORES
    places = sent_ref.shape[0] // CORES
    parts = places // (capacity + 1)
    tiles = tiles_ref.shape[0] // CORES
    copies = []
    for core in range(CORES):
        for slot in range(capacity + 1):
            held = core * capacity + min(slot, capacity - 1)
            if slot < capacity:
                keep = used_ref[held] > 0
                for half in range(CORES):
                    group = lax.rem(column_ref[held] + half, CORES)
                    for tile in range(tiles):
                        rows, lanes = tile_of(tile)
                        lanes = pl.ds(half * width + lanes.start, LANES)
                        value = tiles_ref[group * tiles + tile, held]
                        rows_ref[held, rows, lanes] = jnp.where(keep, value, jnp.zeros_like(value))
            for member in range(parts):
                place = core * places + slot * parts + member
                copies.append(
                    pltpu.make_async_copy(rows_ref.at[held], sent_ref.at[place], sems.at[place])
                )
                copies[-1].start()
    for copy in copies:
        copy.wait()


def held_rows(column_of, used, tiles, height, width, places):
    return pl.pallas_call(
        held_rows_kernel,
        out_shape=jax.ShapeDtypeStruct((places, height, CORES * width), tiles.dtype),
        in_specs=[SMEM, SMEM, VMEM],
        out_specs=pl.BlockSpec(memory_space=pltpu.HBM),
        scratch_shapes=[
            pltpu.VMEM((tiles.shape[1], height, CORES * width), tiles.dtype),
            pltpu.SemaphoreType.DMA((places,)),
        ],
        compiler_params=pltpu.CompilerParams(vmem_limit_bytes=56 * 2**20),
        cost_estimate=cost(0, 4 * 2**20),
    )(column_of, used, tiles)


def three_parts(value):
    high = value.astype(jnp.bfloat16)
    rest = value - high.astype(jnp.float32)
    middle = rest.astype(jnp.bfloat16)
    return [high, middle, (rest - middle.astype(jnp.float32)).astype(jnp.bfloat16)]


def around(place, step, count):
    return lax.rem(place + count - step, count)


def turn_kernel(side, place_ref, root_ref, out_ref):
    x = place_ref[1]
    block_side = root_ref.shape[2]
    width, narrow = block_side // side, block_side // side // side
    for slot in range(root_ref.shape[0]):
        for column in range(side):
            chunk = [
                root_ref[slot, :, pl.ds(row * width + column * narrow, narrow)]
                for row in range(side)
            ]
            lanes = pl.ds(pl.multiple_of(around(column, x, side) * width, width), width)
            out_ref[slot, :, lanes] = jnp.concatenate(chunk, axis=1)


def whole_root_kernel(side, place_ref, own_ref, before_ref, behind_ref, far_ref, out_ref, turned_ref):
    y, x = place_ref[0], place_ref[1]
    block_side = own_ref.shape[2]
    width, narrow = block_side // side, block_side // side // side

    def block(ref, number):
        return jnp.concatenate(
            [
                ref[around(y, at, side), :, pl.ds(number * width, width)]
                for at in range(side)
            ],
            axis=0,
        )

    given = {(0, 0): block(own_ref, 0)}
    for number in range(1, side):
        given[0, number] = block(own_ref, number)
    given[3, 3], given[3, 1], given[3, 2] = (block(before_ref, number) for number in range(3))
    given[1, 1], given[1, 2] = (block(behind_ref, number) for number in range(2))
    given[2, 2] = block(far_ref, 0)
    for first in range(side):
        for second in range(side):
            if (first, second) in given:
                value = given[first, second]
            else:
                value = given[second, first].astype(jnp.float32).T.astype(own_ref.dtype)
            turned_ref[pl.ds(first * width, width), pl.ds(second * width, width)] = value
    for first in range(side):
        rows = pl.ds(first * width, width)
        for column in range(side):
            lanes = pl.ds(pl.multiple_of(around(column, x, side) * width, width), width)
            chunk = turned_ref[rows, lanes]
            for row in range(side):
                out_ref[rows, pl.ds(row * width + column * narrow, narrow)] = chunk[
                    :, row * narrow : (row + 1) * narrow
                ]


def join_kernel(block_ref, out_ref):
    places = block_ref.shape[0] // CORES
    height, width = block_ref.shape[1], block_ref.shape[2] // CORES
    for place in range(places):
        for part in range(out_ref.shape[1] // width):
            out_ref[pl.ds(place * height, height), pl.ds(part * width, width)] = block_ref[
                part % CORES * places + place, :, pl.ds(part // CORES * width, width)
            ]


def precondition_kernel(side, place_ref, left_ref, right_ref, block_ref, out_ref):
    y, x = place_ref[0], place_ref[1]
    places, height, block_side = left_ref.shape
    width = block_side // side
    cores = out_ref.shape[0] // places
    narrow = width // side
    block = jnp.concatenate(
        [
            block_ref[
                pl.ds(part % cores * places, places), :, pl.ds(part // cores * width, width)
            ].reshape(block_side, width)
            for part in range(side)
        ],
        axis=1,
    )
    right = jnp.concatenate([right_ref[around(y, at, side)] for at in range(side)], axis=0)
    power = jnp.zeros((1, width), jnp.float32)
    for begin in range(0, places, side):
        left = left_ref[pl.ds(begin, side)].reshape(side * height, block_side)
        mixed = jnp.dot(left, block, preferred_element_type=jnp.float32).astype(jnp.bfloat16)
        product = lax.dot_general(
            mixed, right, (((1,), (1,)), ((), ())), preferred_element_type=jnp.float32
        )
        power += jnp.sum(product * product, axis=0, keepdims=True)
        product = product.astype(jnp.bfloat16)
        for core in range(cores):
            share = jnp.concatenate(
                [
                    product[:, part * narrow : (part + 1) * narrow]
                    for part in range(core, side, cores)
                ],
                axis=1,
            )
            for at in range(side):
                place = core * places + at * side + lax.rem(x + begin // side, side)
                out_ref[place, pl.ds(0, height), :] = share[at * height : (at + 1) * height]
    share = places // side
    grad = jnp.zeros((1, LANES), jnp.float32)
    for core in range(cores):
        own = block_ref[pl.ds(core * places + x * share, share)].astype(jnp.float32)
        own = own.reshape(width, cores * width)
        own = jnp.sum(own * own, axis=0, keepdims=True)
        grad += sum(own[:, at : at + LANES] for at in range(0, cores * width, LANES))
    power = sum(power[:, at : at + LANES] for at in range(0, width, LANES))
    number = lax.broadcasted_iota(jnp.int32, (TAIL, LANES), 0)
    tail = jnp.zeros((TAIL, LANES), jnp.float32)
    for at, line in enumerate(three_parts(power) + three_parts(grad)):
        tail = jnp.where(number == at, line.astype(jnp.float32), tail)
    tail = tail.astype(jnp.bfloat16)
    for place in range(places * cores):
        out_ref[place, pl.ds(height, TAIL), :] = tail


def precondition(place, left, right, block):
    places, height, block_side = left.shape
    side = right.shape[0]
    width = block_side // side
    return pl.pallas_call(
        functools.partial(precondition_kernel, side),
        out_shape=jax.ShapeDtypeStruct((places * CORES, height + TAIL, LANES), jnp.bfloat16),
        in_specs=[SMEM] + [VMEM] * 3,
        out_specs=VMEM,
        compiler_params=pltpu.CompilerParams(vmem_limit_bytes=20 * 2**20),
        cost_estimate=cost(2 * block_side * block_side * (block_side + width), 6 * 2**20),
    )(place, left, right, block)


def steps_kernel(side, column_ref, back_ref, out_ref):
    height = back_ref.shape[1] - TAIL
    tiles = out_ref.shape[0] // CORES
    narrow = back_ref.shape[2] // CORES
    slots = column_ref.shape[0]
    for held in range(slots):
        core, slot = held // (slots // CORES), held % (slots // CORES)
        first = core * (back_ref.shape[0] // CORES) + slot * side
        sums = sum(
            back_ref[first + member, pl.ds(height, TAIL), :].astype(jnp.float32)
            for member in range(side)
        )
        sums = jnp.sum(sums, axis=1, keepdims=True)
        power = jnp.sum(sums[0:3], axis=0, keepdims=True)
        grad = jnp.sum(sums[3:6], axis=0, keepdims=True)
        scale = -STEP * jnp.sqrt(grad) * lax.rsqrt(power + EPS)
        rows_of = [
            (scale * back_ref[first + member, pl.ds(0, height), :].astype(jnp.float32)).astype(
                jnp.bfloat16
            )
            for member in range(side)
        ]
        for half in range(CORES):
            group = lax.rem(column_ref[held] + half, CORES)
            chunk = jnp.concatenate(
                [rows[:, half * narrow : (half + 1) * narrow] for rows in rows_of], axis=1
            )
            for tile in range(tiles):
                rows, lanes = tile_of(tile)
                out_ref[group * tiles + tile, held] = chunk[
                    rows.start : rows.start + ROWS, lanes.start : lanes.start + LANES
                ]


def update_kernel(half_ref, tiles_ref, out_ref):
    tiles = tiles_ref.shape[0] // CORES
    for column in range(out_ref.shape[0]):
        group = lax.rem(column + half_ref[0], CORES)
        for tile in range(tiles):
            rows, lanes = tile_of(tile)
            out_ref[column, rows, lanes] = tiles_ref[group * tiles + tile, column // CORES]


def statistics_kernel(side, place_ref, left_ref, right_ref, *refs):
    term_refs, outs = refs[:side], refs[side:]
    for step in range(side):
        slot = around(place_ref[0], step, side)

        @pl.when(slot < left_ref.shape[0])
        def _():
            for kind, (old, new) in enumerate(zip((left_ref, right_ref), outs)):
                term = term_refs[step][kind].astype(jnp.float32)
                new[slot] = BETA * old[slot] + (1.0 - BETA) * term


def per_device(gradient, block_owner, left_stats, right_stats, left_root, right_root):
    tensor_index = lax.axis_index("tensor")
    fsdp_index = lax.axis_index("fsdp")
    fsdp_count = lax.axis_size("fsdp")
    tensor_count = lax.axis_size("tensor")
    col_blocks, local_height, row_depth = gradient.shape
    row_blocks = block_owner.shape[1]
    capacity, _, block_side = left_stats.shape
    side = block_side // row_depth
    y, x = tensor_index // side, tensor_index % side
    place = jnp.stack([y, x]).astype(jnp.int32)

    def along_y(value, step, sources, targets):
        pairs = [
            (a * side + b, (a + step) % side * side + b)
            for a in range(side)
            for b in range(side)
            if a < sources and (a + step) % side < targets
        ]
        return lax.ppermute(value, "tensor", pairs)

    def along_x(value, step, rows):
        pairs = [
            (a * side + b, a * side + (b + step) % side) for a in range(rows) for b in range(side)
        ]
        return lax.ppermute(value, "tensor", pairs)

    chips = fsdp_count // CORES

    def along_z(value):
        rings = [[chip * CORES + core for chip in range(chips)] for core in range(CORES)]
        return lax.all_to_all(
            value, "fsdp", split_axis=0, concat_axis=0, tiled=True, axis_index_groups=rings
        )

    def over_chip_planes(value):
        count = CORES * tensor_count
        planes = [[chip * count + member for member in range(count)] for chip in range(chips)]
        return lax.all_to_all(
            value,
            ("fsdp", "tensor"),
            split_axis=0,
            concat_axis=0,
            tiled=True,
            axis_index_groups=planes,
        )

    chip = fsdp_index // CORES
    group = chip // (chips // CORES)
    half_here = (chip % CORES).astype(jnp.int32).reshape(1)

    with jax.named_scope("gradient_spread"):
        spread = pl.pallas_call(
            spread_kernel,
            out_shape=jax.ShapeDtypeStruct(
                (chips, col_blocks // CORES, ROWS, LANES), gradient.dtype
            ),
            in_specs=[SMEM, VMEM],
            out_specs=VMEM,
            compiler_params=LIMIT,
            cost_estimate=cost(0, 2**18),
        )(half_here, gradient)
        spread, left_root, right_root = lax.optimization_barrier((spread, left_root, right_root))
        spread = along_z(spread).reshape(-1, ROWS, LANES)

    with jax.named_scope("where_blocks_go"):
        owners_flat = block_owner.reshape(-1)
        numbers = jnp.arange(owners_flat.shape[0])
        column_flat, band_flat = numbers // row_blocks, numbers % row_blocks
        entries = owners_flat * capacity + slot_numbers(owners_flat)
        held_at = entries[:, None] == jnp.arange(fsdp_count * capacity)[None, :]
        source = band_flat * CORES + (group - column_flat % CORES + CORES) % CORES
        source = source * (col_blocks // CORES) + column_flat // CORES
        forward = jnp.sum(jnp.where(held_at, source[:, None], 0), axis=0).astype(jnp.int32)
        ours = (chip * CORES * capacity + jnp.arange(CORES * capacity))[None, :]
        ours = entries[:, None] == ours
        used = jnp.any(ours, axis=0).astype(jnp.int32)
        columns_here = jnp.sum(jnp.where(ours, column_flat[:, None], 0), axis=0).astype(jnp.int32)
        homes = jnp.arange(chips)[:, None]
        turn = (group - homes % CORES + CORES) % CORES
        wanted = CORES * jnp.arange(col_blocks // CORES)[None, :] + turn
        wanted = (wanted * row_blocks + homes // CORES).reshape(-1)
        backward = jnp.sum(
            jnp.where(wanted[:, None] == numbers[None, :], entries[None, :], 0), axis=1
        ).astype(jnp.int32)

    with jax.named_scope("gradient_to_owners"):
        sent = pick(forward, spread).reshape(chips, CORES * capacity, ROWS, LANES)
        tiles = along_z(sent)

    with jax.named_scope("roots_to_slot_groups"):
        turned = pl.pallas_call(
            functools.partial(turn_kernel, side),
            out_shape=jax.ShapeDtypeStruct(left_root.shape, left_root.dtype),
            in_specs=[SMEM, VMEM],
            out_specs=VMEM,
            compiler_params=LIMIT,
            cost_estimate=cost(0, 2**20),
        )(place, left_root)
        roots = jnp.stack([turned, right_root], axis=1)
        taken = []
        for step in range(side):
            slot = jnp.minimum((y + step) % side, capacity - 1)
            own = lax.dynamic_index_in_dim(roots, slot, 0, keepdims=False)
            taken.append(along_y(own, step, side, capacity) if step else own)
        left_rows = jnp.stack([piece[0] for piece in taken])
        right_rows = jnp.stack([piece[1] for piece in taken])
        width = row_depth
        lefts = [
            left_rows,
            along_x(
                jnp.concatenate([left_rows[:, :, :width], left_rows[:, :, 2 * width :]], axis=2),
                1,
                capacity,
            ),
            along_x(left_rows[:, :, : 2 * width], side - 1, capacity),
            along_x(left_rows[:, :, :width], 2, capacity),
        ]
        tiles, right_rows, *lefts = lax.optimization_barrier((tiles, right_rows, *lefts))

    with jax.named_scope("rows_of_held_blocks"):
        sent = held_rows(
            columns_here, used, tiles, local_height, row_depth, CORES * tensor_count
        )
        sent, *lefts = lax.optimization_barrier((sent, *lefts))
        block = over_chip_planes(sent)
        left = pl.pallas_call(
            functools.partial(whole_root_kernel, side),
            out_shape=jax.ShapeDtypeStruct((block_side, block_side), left_root.dtype),
            in_specs=[SMEM] + [VMEM] * len(lefts),
            out_specs=VMEM,
            scratch_shapes=[pltpu.VMEM((block_side, block_side), left_root.dtype)],
            compiler_params=LIMIT,
            cost_estimate=cost(0, 8 * 2**20),
        )(place, *lefts)
        left = left.reshape(tensor_count, local_height, block_side)

    with jax.named_scope("precondition"):
        leaving = precondition(place, left, right_rows, block)

    with jax.named_scope("step_to_gradient_rows"):
        back = over_chip_planes(leaving)
        block, leaving = lax.optimization_barrier((block, leaving))
        block = pl.pallas_call(
            join_kernel,
            out_shape=jax.ShapeDtypeStruct((block_side, block_side), block.dtype),
            in_specs=[VMEM],
            out_specs=VMEM,
            compiler_params=LIMIT,
            cost_estimate=cost(0, 4 * 2**20),
        )(block)
        own_rows = lax.dynamic_index_in_dim(
            block.reshape(side, side, local_height, block_side), x, 1, keepdims=False
        ).reshape(row_depth, block_side)
        own_columns = jnp.concatenate(
            [
                lax.dynamic_slice_in_dim(block, (at * side + x) * local_height, local_height, 1)
                for at in range(side)
            ],
            axis=1,
        )
        left_term = jnp.einsum("ak,jk->aj", own_rows, block, preferred_element_type=jnp.float32)
        right_term = jnp.einsum("ja,jk->ak", own_columns, block, preferred_element_type=jnp.float32)
        terms = jnp.stack([left_term.astype(jnp.bfloat16), right_term.astype(jnp.bfloat16)])
        terms = terms.reshape(2, side, local_height, block_side)
        terms = [
            lax.dynamic_index_in_dim(terms, (y + step) % side, 1, keepdims=False)
            for step in range(side)
        ]
        back, *terms = lax.optimization_barrier((back, *terms))
        steps = pl.pallas_call(
            functools.partial(steps_kernel, side),
            out_shape=jax.ShapeDtypeStruct((chips, CORES * capacity, ROWS, LANES), jnp.bfloat16),
            in_specs=[SMEM, VMEM],
            out_specs=VMEM,
            compiler_params=LIMIT,
            cost_estimate=cost(0, 2 * 2**20),
        )(columns_here, back)
        steps, *terms = lax.optimization_barrier((steps, *terms))
        passing = along_z(steps).reshape(fsdp_count * capacity, ROWS, LANES)

    with jax.named_scope("statistics"):
        arrived = terms[:1] + [
            along_y(terms[step], step, capacity, side) for step in range(1, side)
        ]
        passing, *arrived = lax.optimization_barrier((passing, *arrived))
        returned = along_z(
            pick(backward, passing).reshape(chips, col_blocks // CORES, ROWS, LANES)
        )
        left_updated, right_updated = pl.pallas_call(
            functools.partial(statistics_kernel, side),
            out_shape=(
                jax.ShapeDtypeStruct(left_stats.shape, left_stats.dtype),
                jax.ShapeDtypeStruct(right_stats.shape, right_stats.dtype),
            ),
            in_specs=[SMEM] + [VMEM] * (2 + side),
            out_specs=(VMEM, VMEM),
            compiler_params=LIMIT,
            cost_estimate=cost(0, 4 * 2**20),
        )(place, left_stats, right_stats, *arrived)
        returned, left_updated, right_updated = lax.optimization_barrier(
            (returned, left_updated, right_updated)
        )

    with jax.named_scope("update"):
        update = pl.pallas_call(
            update_kernel,
            out_shape=jax.ShapeDtypeStruct(gradient.shape, gradient.dtype),
            in_specs=[SMEM, VMEM],
            out_specs=VMEM,
            compiler_params=LIMIT,
            cost_estimate=cost(0, 2**20),
        )(half_here, returned)
    return (left_updated, right_updated, update)


def solution(mesh):
    placed = (
        P(None, "tensor", "fsdp"),
        P(),
        P("fsdp", "tensor", None),
        P("fsdp", "tensor", None),
        P("fsdp", "tensor", None),
        P("fsdp", "tensor", None),
    )
    return jax.shard_map(
        per_device,
        mesh=mesh,
        in_specs=placed,
        out_specs=(P("fsdp", "tensor", None), P("fsdp", "tensor", None), P(None, "tensor", "fsdp")),
        check_vma=False,
    )
```

```python
import functools
import jax
import jax.numpy as jnp
from jax import lax
from jax.experimental import pallas as pl
from jax.experimental.pallas import tpu as pltpu
from jax.sharding import PartitionSpec as P

BETA = 0.999
STEP = 0.5
EPS = 1e-06
TAIL = 16
ROWS = 16
LANES = 128
CORES = 2
VMEM = pl.BlockSpec(memory_space=pltpu.VMEM)
ANY = pl.BlockSpec(memory_space=pl.ANY)
SMEM = pl.BlockSpec(memory_space=pltpu.SMEM)
LIMIT = pltpu.CompilerParams(vmem_limit_bytes=24 * 2**20)


def cost(flops, moved):
    return pl.CostEstimate(flops=flops, bytes_accessed=moved, transcendentals=0)


def slot_numbers(owners_flat):
    total = owners_flat.shape[0]
    same = owners_flat[:, None] == owners_flat[None, :]
    earlier = jnp.arange(total)[None, :] < jnp.arange(total)[:, None]
    return jnp.sum(jnp.where(same & earlier, 1, 0), axis=1).astype(jnp.int32)


def tile_of(number):
    return pl.ds(number // 2 * ROWS, ROWS), pl.ds(number % 2 * LANES, LANES)


def spread_kernel(half_ref, gradient_ref, out_ref):
    tiles = out_ref.shape[0] // CORES
    for group in range(CORES):
        for pair in range(out_ref.shape[1]):
            column = CORES * pair + lax.rem(group + CORES - half_ref[0], CORES)
            for tile in range(tiles):
                rows, lanes = tile_of(tile)
                out_ref[group * tiles + tile, pair] = gradient_ref[column, rows, lanes]


def pick_kernel(index_ref, tiles_ref, out_ref):
    for at in range(out_ref.shape[0]):
        out_ref[at] = tiles_ref[index_ref[at]]


def pick(index, tiles):
    shape = (index.shape[0],) + tiles.shape[1:]
    return pl.pallas_call(
        pick_kernel,
        out_shape=jax.ShapeDtypeStruct(shape, tiles.dtype),
        in_specs=[SMEM, VMEM],
        out_specs=VMEM,
        compiler_params=LIMIT,
        cost_estimate=cost(0, 2**20),
    )(index, tiles)


def held_rows_kernel(column_ref, used_ref, tiles_ref, sent_ref, rows_ref, sems):
    capacity = rows_ref.shape[0] // CORES
    width = rows_ref.shape[2] // CORES
    places = sent_ref.shape[0] // CORES
    parts = places // (capacity + 1)
    tiles = tiles_ref.shape[0] // CORES
    copies = []
    for core in range(CORES):
        for slot in range(capacity + 1):
            held = core * capacity + min(slot, capacity - 1)
            if slot < capacity:
                keep = used_ref[held] > 0
                for half in range(CORES):
                    group = lax.rem(column_ref[held] + half, CORES)
                    for tile in range(tiles):
                        rows, lanes = tile_of(tile)
                        lanes = pl.ds(half * width + lanes.start, LANES)
                        value = tiles_ref[group * tiles + tile, held]
                        rows_ref[held, rows, lanes] = jnp.where(keep, value, jnp.zeros_like(value))
            for member in range(parts):
                place = core * places + slot * parts + member
                copies.append(
                    pltpu.make_async_copy(rows_ref.at[held], sent_ref.at[place], sems.at[place])
                )
                copies[-1].start()
    for copy in copies:
        copy.wait()


def held_rows(column_of, used, tiles, height, width, places):
    return pl.pallas_call(
        held_rows_kernel,
        out_shape=jax.ShapeDtypeStruct((places, height, CORES * width), tiles.dtype),
        in_specs=[SMEM, SMEM, VMEM],
        out_specs=pl.BlockSpec(memory_space=pltpu.HBM),
        scratch_shapes=[
            pltpu.VMEM((tiles.shape[1], height, CORES * width), tiles.dtype),
            pltpu.SemaphoreType.DMA((places,)),
        ],
        compiler_params=pltpu.CompilerParams(vmem_limit_bytes=56 * 2**20),
        cost_estimate=cost(0, 4 * 2**20),
    )(column_of, used, tiles)


def three_parts(value):
    high = value.astype(jnp.bfloat16)
    rest = value - high.astype(jnp.float32)
    middle = rest.astype(jnp.bfloat16)
    return [high, middle, (rest - middle.astype(jnp.float32)).astype(jnp.bfloat16)]


def around(place, step, count):
    return lax.rem(place + count - step, count)


def turn_kernel(side, place_ref, root_ref, out_ref):
    x = place_ref[1]
    block_side = root_ref.shape[2]
    width, narrow = block_side // side, block_side // side // side
    for slot in range(root_ref.shape[0]):
        for column in range(side):
            chunk = [
                root_ref[slot, :, pl.ds(row * width + column * narrow, narrow)]
                for row in range(side)
            ]
            lanes = pl.ds(pl.multiple_of(around(column, x, side) * width, width), width)
            out_ref[slot, :, lanes] = jnp.concatenate(chunk, axis=1)


def whole_root_kernel(side, place_ref, own_ref, before_ref, behind_ref, far_ref, out_ref, turned_ref):
    y, x = place_ref[0], place_ref[1]
    block_side = own_ref.shape[2]
    width, narrow = block_side // side, block_side // side // side

    def block(ref, number):
        return jnp.concatenate(
            [
                ref[around(y, at, side), :, pl.ds(number * width, width)]
                for at in range(side)
            ],
            axis=0,
        )

    given = {(0, 0): block(own_ref, 0)}
    for number in range(1, side):
        given[0, number] = block(own_ref, number)
    given[3, 3], given[3, 1], given[3, 2] = (block(before_ref, number) for number in range(3))
    given[1, 1], given[1, 2] = (block(behind_ref, number) for number in range(2))
    given[2, 2] = block(far_ref, 0)
    for first in range(side):
        for second in range(side):
            if (first, second) in given:
                value = given[first, second]
            else:
                value = given[second, first].astype(jnp.float32).T.astype(own_ref.dtype)
            turned_ref[pl.ds(first * width, width), pl.ds(second * width, width)] = value
    for first in range(side):
        rows = pl.ds(first * width, width)
        for column in range(side):
            lanes = pl.ds(pl.multiple_of(around(column, x, side) * width, width), width)
            chunk = turned_ref[rows, lanes]
            for row in range(side):
                out_ref[rows, pl.ds(row * width + column * narrow, narrow)] = chunk[
                    :, row * narrow : (row + 1) * narrow
                ]


def join_kernel(block_ref, out_ref):
    places = block_ref.shape[0] // CORES
    height, width = block_ref.shape[1], block_ref.shape[2] // CORES
    for place in range(places):
        for part in range(out_ref.shape[1] // width):
            out_ref[pl.ds(place * height, height), pl.ds(part * width, width)] = block_ref[
                part % CORES * places + place, :, pl.ds(part // CORES * width, width)
            ]


def precondition_kernel(side, place_ref, left_ref, right_ref, block_ref, out_ref):
    y, x = place_ref[0], place_ref[1]
    places, height, block_side = left_ref.shape
    width = block_side // side
    cores = out_ref.shape[0] // places
    narrow = width // side
    block = jnp.concatenate(
        [
            block_ref[
                pl.ds(part % cores * places, places), :, pl.ds(part // cores * width, width)
            ].reshape(block_side, width)
            for part in range(side)
        ],
        axis=1,
    )
    right = jnp.concatenate([right_ref[around(y, at, side)] for at in range(side)], axis=0)
    mixed = lax.dot_general(
        block, right, (((1,), (1,)), ((), ())), preferred_element_type=jnp.float32
    ).astype(jnp.bfloat16)
    power = jnp.zeros((1, width), jnp.float32)
    for begin in range(0, places, side):
        left = left_ref[pl.ds(begin, side)].reshape(side * height, block_side)
        product = jnp.dot(left, mixed, preferred_element_type=jnp.float32)
        power += jnp.sum(product * product, axis=0, keepdims=True)
        product = product.astype(jnp.bfloat16)
        for core in range(cores):
            share = jnp.concatenate(
                [
                    product[:, part * narrow : (part + 1) * narrow]
                    for part in range(core, side, cores)
                ],
                axis=1,
            )
            for at in range(side):
                place = core * places + at * side + lax.rem(x + begin // side, side)
                out_ref[place, pl.ds(0, height), :] = share[at * height : (at + 1) * height]
    share = places // side
    grad = jnp.zeros((1, LANES), jnp.float32)
    for core in range(cores):
        own = block_ref[pl.ds(core * places + x * share, share)].astype(jnp.float32)
        own = own.reshape(width, cores * width)
        own = jnp.sum(own * own, axis=0, keepdims=True)
        grad += sum(own[:, at : at + LANES] for at in range(0, cores * width, LANES))
    power = sum(power[:, at : at + LANES] for at in range(0, width, LANES))
    number = lax.broadcasted_iota(jnp.int32, (TAIL, LANES), 0)
    tail = jnp.zeros((TAIL, LANES), jnp.float32)
    for at, line in enumerate(three_parts(power) + three_parts(grad)):
        tail = jnp.where(number == at, line.astype(jnp.float32), tail)
    tail = tail.astype(jnp.bfloat16)
    for place in range(places * cores):
        out_ref[place, pl.ds(height, TAIL), :] = tail


def precondition(place, left, right, block):
    places, height, block_side = left.shape
    side = right.shape[0]
    width = block_side // side
    return pl.pallas_call(
        functools.partial(precondition_kernel, side),
        out_shape=jax.ShapeDtypeStruct((places * CORES, height + TAIL, LANES), jnp.bfloat16),
        in_specs=[SMEM] + [VMEM] * 3,
        out_specs=VMEM,
        compiler_params=pltpu.CompilerParams(vmem_limit_bytes=20 * 2**20),
        cost_estimate=cost(2 * block_side * block_side * (block_side + width), 6 * 2**20),
    )(place, left, right, block)


def steps_kernel(side, column_ref, back_ref, out_ref):
    height = back_ref.shape[1] - TAIL
    tiles = out_ref.shape[0] // CORES
    narrow = back_ref.shape[2] // CORES
    slots = column_ref.shape[0]
    for held in range(slots):
        core, slot = held // (slots // CORES), held % (slots // CORES)
        first = core * (back_ref.shape[0] // CORES) + slot * side
        sums = sum(
            back_ref[first + member, pl.ds(height, TAIL), :].astype(jnp.float32)
            for member in range(side)
        )
        sums = jnp.sum(sums, axis=1, keepdims=True)
        power = jnp.sum(sums[0:3], axis=0, keepdims=True)
        grad = jnp.sum(sums[3:6], axis=0, keepdims=True)
        scale = -STEP * jnp.sqrt(grad) * lax.rsqrt(power + EPS)
        rows_of = [
            (scale * back_ref[first + member, pl.ds(0, height), :].astype(jnp.float32)).astype(
                jnp.bfloat16
            )
            for member in range(side)
        ]
        for half in range(CORES):
            group = lax.rem(column_ref[held] + half, CORES)
            chunk = jnp.concatenate(
                [rows[:, half * narrow : (half + 1) * narrow] for rows in rows_of], axis=1
            )
            for tile in range(tiles):
                rows, lanes = tile_of(tile)
                out_ref[group * tiles + tile, held] = chunk[
                    rows.start : rows.start + ROWS, lanes.start : lanes.start + LANES
                ]


def update_kernel(half_ref, tiles_ref, out_ref):
    tiles = tiles_ref.shape[0] // CORES
    for column in range(out_ref.shape[0]):
        group = lax.rem(column + half_ref[0], CORES)
        for tile in range(tiles):
            rows, lanes = tile_of(tile)
            out_ref[column, rows, lanes] = tiles_ref[group * tiles + tile, column // CORES]


def statistics_kernel(side, place_ref, left_ref, right_ref, *refs):
    term_refs, outs = refs[:side], refs[side:]
    for step in range(side):
        slot = around(place_ref[0], step, side)

        @pl.when(slot < left_ref.shape[0])
        def _():
            for kind, (old, new) in enumerate(zip((left_ref, right_ref), outs)):
                term = term_refs[step][kind].astype(jnp.float32)
                new[slot] = BETA * old[slot] + (1.0 - BETA) * term


def per_device(gradient, block_owner, left_stats, right_stats, left_root, right_root):
    tensor_index = lax.axis_index("tensor")
    fsdp_index = lax.axis_index("fsdp")
    fsdp_count = lax.axis_size("fsdp")
    tensor_count = lax.axis_size("tensor")
    col_blocks, local_height, row_depth = gradient.shape
    row_blocks = block_owner.shape[1]
    capacity, _, block_side = left_stats.shape
    side = block_side // row_depth
    y, x = tensor_index // side, tensor_index % side
    place = jnp.stack([y, x]).astype(jnp.int32)

    def along_y(value, step, sources, targets):
        pairs = [
            (a * side + b, (a + step) % side * side + b)
            for a in range(side)
            for b in range(side)
            if a < sources and (a + step) % side < targets
        ]
        return lax.ppermute(value, "tensor", pairs)

    def along_x(value, step, rows):
        pairs = [
            (a * side + b, a * side + (b + step) % side) for a in range(rows) for b in range(side)
        ]
        return lax.ppermute(value, "tensor", pairs)

    chips = fsdp_count // CORES

    def along_z(value):
        rings = [[chip * CORES + core for chip in range(chips)] for core in range(CORES)]
        return lax.all_to_all(
            value, "fsdp", split_axis=0, concat_axis=0, tiled=True, axis_index_groups=rings
        )

    def over_chip_planes(value):
        count = CORES * tensor_count
        planes = [[chip * count + member for member in range(count)] for chip in range(chips)]
        return lax.all_to_all(
            value,
            ("fsdp", "tensor"),
            split_axis=0,
            concat_axis=0,
            tiled=True,
            axis_index_groups=planes,
        )

    chip = fsdp_index // CORES
    group = chip // (chips // CORES)
    half_here = (chip % CORES).astype(jnp.int32).reshape(1)

    with jax.named_scope("gradient_spread"):
        spread = pl.pallas_call(
            spread_kernel,
            out_shape=jax.ShapeDtypeStruct(
                (chips, col_blocks // CORES, ROWS, LANES), gradient.dtype
            ),
            in_specs=[SMEM, VMEM],
            out_specs=VMEM,
            compiler_params=LIMIT,
            cost_estimate=cost(0, 2**18),
        )(half_here, gradient)
        spread, left_root, right_root = lax.optimization_barrier((spread, left_root, right_root))
        spread = along_z(spread).reshape(-1, ROWS, LANES)

    with jax.named_scope("where_blocks_go"):
        owners_flat = block_owner.reshape(-1)
        numbers = jnp.arange(owners_flat.shape[0])
        column_flat, band_flat = numbers // row_blocks, numbers % row_blocks
        entries = owners_flat * capacity + slot_numbers(owners_flat)
        held_at = entries[:, None] == jnp.arange(fsdp_count * capacity)[None, :]
        source = band_flat * CORES + (group - column_flat % CORES + CORES) % CORES
        source = source * (col_blocks // CORES) + column_flat // CORES
        forward = jnp.sum(jnp.where(held_at, source[:, None], 0), axis=0).astype(jnp.int32)
        ours = (chip * CORES * capacity + jnp.arange(CORES * capacity))[None, :]
        ours = entries[:, None] == ours
        used = jnp.any(ours, axis=0).astype(jnp.int32)
        columns_here = jnp.sum(jnp.where(ours, column_flat[:, None], 0), axis=0).astype(jnp.int32)
        homes = jnp.arange(chips)[:, None]
        turn = (group - homes % CORES + CORES) % CORES
        wanted = CORES * jnp.arange(col_blocks // CORES)[None, :] + turn
        wanted = (wanted * row_blocks + homes // CORES).reshape(-1)
        backward = jnp.sum(
            jnp.where(wanted[:, None] == numbers[None, :], entries[None, :], 0), axis=1
        ).astype(jnp.int32)

    with jax.named_scope("gradient_to_owners"):
        sent = pick(forward, spread).reshape(chips, CORES * capacity, ROWS, LANES)
        tiles = along_z(sent)

    with jax.named_scope("roots_to_slot_groups"):
        turned = pl.pallas_call(
            functools.partial(turn_kernel, side),
            out_shape=jax.ShapeDtypeStruct(left_root.shape, left_root.dtype),
            in_specs=[SMEM, VMEM],
            out_specs=VMEM,
            compiler_params=LIMIT,
            cost_estimate=cost(0, 2**20),
        )(place, left_root)
        roots = jnp.stack([turned, right_root], axis=1)
        taken = []
        for step in range(side):
            slot = jnp.minimum((y + step) % side, capacity - 1)
            own = lax.dynamic_index_in_dim(roots, slot, 0, keepdims=False)
            taken.append(along_y(own, step, side, capacity) if step else own)
        left_rows = jnp.stack([piece[0] for piece in taken])
        right_rows = jnp.stack([piece[1] for piece in taken])
        width = row_depth
        lefts = [
            left_rows,
            along_x(
                jnp.concatenate([left_rows[:, :, :width], left_rows[:, :, 2 * width :]], axis=2),
                1,
                capacity,
            ),
            along_x(left_rows[:, :, : 2 * width], side - 1, capacity),
            along_x(left_rows[:, :, :width], 2, capacity),
        ]
        tiles, right_rows, *lefts = lax.optimization_barrier((tiles, right_rows, *lefts))

    with jax.named_scope("rows_of_held_blocks"):
        sent = held_rows(
            columns_here, used, tiles, local_height, row_depth, CORES * tensor_count
        )
        sent, *lefts = lax.optimization_barrier((sent, *lefts))
        block = over_chip_planes(sent)
        left = pl.pallas_call(
            functools.partial(whole_root_kernel, side),
            out_shape=jax.ShapeDtypeStruct((block_side, block_side), left_root.dtype),
            in_specs=[SMEM] + [VMEM] * len(lefts),
            out_specs=VMEM,
            scratch_shapes=[pltpu.VMEM((block_side, block_side), left_root.dtype)],
            compiler_params=LIMIT,
            cost_estimate=cost(0, 8 * 2**20),
        )(place, *lefts)
        left = left.reshape(tensor_count, local_height, block_side)

    with jax.named_scope("precondition"):
        leaving = precondition(place, left, right_rows, block)

    with jax.named_scope("step_to_gradient_rows"):
        back = over_chip_planes(leaving)
        block, leaving = lax.optimization_barrier((block, leaving))
        block = pl.pallas_call(
            join_kernel,
            out_shape=jax.ShapeDtypeStruct((block_side, block_side), block.dtype),
            in_specs=[VMEM],
            out_specs=VMEM,
            compiler_params=LIMIT,
            cost_estimate=cost(0, 4 * 2**20),
        )(block)
        own_rows = lax.dynamic_index_in_dim(
            block.reshape(side, side, local_height, block_side), x, 1, keepdims=False
        ).reshape(row_depth, block_side)
        own_columns = jnp.concatenate(
            [
                lax.dynamic_slice_in_dim(block, (at * side + x) * local_height, local_height, 1)
                for at in range(side)
            ],
            axis=1,
        )
        left_term = jnp.einsum("ak,jk->aj", own_rows, block, preferred_element_type=jnp.float32)
        right_term = jnp.einsum("ja,jk->ak", own_columns, block, preferred_element_type=jnp.float32)
        terms = jnp.stack([left_term.astype(jnp.bfloat16), right_term.astype(jnp.bfloat16)])
        terms = terms.reshape(2, side, local_height, block_side)
        terms = [
            lax.dynamic_index_in_dim(terms, (y + step) % side, 1, keepdims=False)
            for step in range(side)
        ]
        back, *terms = lax.optimization_barrier((back, *terms))
        steps = pl.pallas_call(
            functools.partial(steps_kernel, side),
            out_shape=jax.ShapeDtypeStruct((chips, CORES * capacity, ROWS, LANES), jnp.bfloat16),
            in_specs=[SMEM, VMEM],
            out_specs=VMEM,
            compiler_params=LIMIT,
            cost_estimate=cost(0, 2 * 2**20),
        )(columns_here, back)
        steps, *terms = lax.optimization_barrier((steps, *terms))
        passing = along_z(steps).reshape(fsdp_count * capacity, ROWS, LANES)

    with jax.named_scope("statistics"):
        arrived = terms[:1] + [
            along_y(terms[step], step, capacity, side) for step in range(1, side)
        ]
        passing, *arrived = lax.optimization_barrier((passing, *arrived))
        returned = along_z(
            pick(backward, passing).reshape(chips, col_blocks // CORES, ROWS, LANES)
        )
        left_updated, right_updated = pl.pallas_call(
            functools.partial(statistics_kernel, side),
            out_shape=(
                jax.ShapeDtypeStruct(left_stats.shape, left_stats.dtype),
                jax.ShapeDtypeStruct(right_stats.shape, right_stats.dtype),
            ),
            in_specs=[SMEM] + [VMEM] * (2 + side),
            out_specs=(VMEM, VMEM),
            compiler_params=LIMIT,
            cost_estimate=cost(0, 4 * 2**20),
        )(place, left_stats, right_stats, *arrived)
        returned, left_updated, right_updated = lax.optimization_barrier(
            (returned, left_updated, right_updated)
        )

    with jax.named_scope("update"):
        update = pl.pallas_call(
            update_kernel,
            out_shape=jax.ShapeDtypeStruct(gradient.shape, gradient.dtype),
            in_specs=[SMEM, VMEM],
            out_specs=VMEM,
            compiler_params=LIMIT,
            cost_estimate=cost(0, 2**20),
        )(half_here, returned)
    return (left_updated, right_updated, update)


def solution(mesh):
    placed = (
        P(None, "tensor", "fsdp"),
        P(),
        P("fsdp", "tensor", None),
        P("fsdp", "tensor", None),
        P("fsdp", "tensor", None),
        P("fsdp", "tensor", None),
    )
    return jax.shard_map(
        per_device,
        mesh=mesh,
        in_specs=placed,
        out_specs=(P("fsdp", "tensor", None), P("fsdp", "tensor", None), P(None, "tensor", "fsdp")),
        check_vma=False,
    )
```
